256 devices in a mesh: tm: 32 (over x, y, core), space: 8 (over z).
Axes of the slice: x: 4, y: 4, z: 8, core: 2. Of those that a mesh axis runs over, the one named last changes fastest.
Arguments:
- frames_in: bfloat16 [256, 32, 64, 256], P('tm', 'space'), may hold values from -6 to 6
- cotangent: bfloat16 [256, 32, 64, 256], P('tm', 'space'), may hold values from -6 to 6
- spatial: bfloat16 [3, 3, 256, 256], replicated, may hold values from -0.125 to 0.125
- temporal: bfloat16 [3, 256, 256], replicated, may hold values from -0.375 to 0.375
- norm_gain: float32 [256], replicated, may hold values from 0.5 to 2
- norm_shift: float32 [256], replicated, may hold values from -3 to 3
- clip_frames: int32 [2], replicated, may hold values from 32 to 216, as said below
- dilation: int32 [2], replicated, may hold values from 1 to 8, as said below
Outputs:
- out_frames: bfloat16 [256, 32, 64, 256], P('tm', 'space')
- in_grad: bfloat16 [256, 32, 64, 256], P('tm', 'space')
- spatial_grad: float32 [3, 3, 256, 256], replicated
- temporal_grad: float32 [3, 256, 256], replicated
The draws below stay inside these ranges and needn't reach their ends.
Inputs may be any that keep to these rules, and one draw needn't show every extreme that they name: `clip_frames`: the two clips are packed in order from slot 0 and fill at least 248 and at most 256 slots together; one of them has exactly 216 frames. One of the two clips has dilation 8.
All inputs are finite; a program needn't handle non-finite values.
Results may differ from the reference program's by a relative error of at most 0.0055.
Values may be sent and summed in bfloat16 or wider, within the bound.
A program may use at most 128 MiB of HBM per device.

```python
import math
import jax
import jax.numpy as jnp
from jax import lax

C = 256
GROUPS = 32
H = 32
W = 64
DMAX = 8
FS = 8
SLOTS = 256


def draw_clip_frames(key, part):
    key = jax.random.fold_in(key, 7)
    short_key, coin_key = jax.random.split(key)
    lowest = SLOTS // 8
    longest = SLOTS - lowest - FS
    shorter = jax.random.randint(short_key, (), lowest, lowest + FS + 1)
    coin_flip = jax.random.randint(coin_key, (), 0, 2)
    longer = jnp.int32(longest)
    return jnp.where(coin_flip == 0, jnp.stack([longer, shorter]), jnp.stack([shorter, longer])).astype(jnp.int32)


def draw_dilation(key, part):
    key = jax.random.fold_in(key, 13)
    coin_key, second_key = jax.random.split(key)
    second = jax.random.randint(second_key, (), 1, DMAX + 1)
    coin_flip = jax.random.randint(coin_key, (), 0, 2)
    widest = jnp.int32(DMAX)
    return jnp.where(coin_flip == 0, jnp.stack([widest, second]), jnp.stack([second, widest])).astype(jnp.int32)


def levels(stream_key, shape, shards, least, largest):
    level, own = 1.0, jax.random.fold_in(stream_key, 6)
    for position, blocks in shards:
        steps = jnp.exp(jax.random.uniform(jax.random.fold_in(own, position), (blocks,), jnp.float32, least / len(shards), largest / len(shards)))
        level = level * jnp.repeat(steps, shape[position] // blocks).reshape([-1 if axis == position else 1 for axis in range(len(shape))])
    return level


def scatter_about(own_key, dims, width, reach, cuts=(), kind=jnp.bfloat16):
    gain = levels(own_key, dims, cuts, -0.22, 0.18) if cuts else 1.0
    values = jax.random.normal(own_key, dims, jnp.float32) * width * gain
    return jnp.minimum(jnp.maximum(values, -reach), reach).astype(kind)


def setup_inputs(seed: int = 0) -> dict:
    arg_keys = jax.random.split(jax.random.key(seed), 9)
    frames_in = scatter_about(arg_keys[0], (SLOTS, H, W, C), 1.0, 6.0, ((0, 32), (1, 8)))
    cotangent = scatter_about(arg_keys[1], (SLOTS, H, W, C), 1.0, 6.0, ((0, 32), (1, 8)))
    spatial = scatter_about(arg_keys[2], (3, 3, C, C), (9 * C) ** -0.5, 0.125)
    temporal = scatter_about(arg_keys[3], (3, C, C), C ** -0.5, 0.375)
    norm_gain = jnp.clip(jnp.exp(jax.random.uniform(arg_keys[4], (C,), jnp.float32, math.log(0.5), math.log(2.0))), 0.5, 2.0)
    norm_shift = scatter_about(arg_keys[5], (C,), 0.5, 3.0, (), jnp.float32)
    clip_frames = draw_clip_frames(jax.random.fold_in(arg_keys[8], 71), 0)
    dilation = draw_dilation(jax.random.fold_in(arg_keys[8], 71), 0)
    return dict(frames_in=frames_in, cotangent=cotangent, spatial=spatial, temporal=temporal, norm_gain=norm_gain, norm_shift=norm_shift, clip_frames=clip_frames, dilation=dilation)


NORM_EPS = 1e-05

def slot_tables(frame_ids, clip_frames):
    filled = clip_frames[0] + clip_frames[1]
    usable = (frame_ids >= 0) & (frame_ids < filled)
    clip_ids = (frame_ids >= clip_frames[0]).astype(jnp.int32)
    return (usable, clip_ids)

def shifted_pieces(source, first_frame, out_first, frame_count, clip_frames, dilation, direction):
    frame_ids = out_first + jnp.arange(frame_count, dtype=jnp.int32)
    usable, clip_ids = slot_tables(frame_ids, clip_frames)
    results = []
    for tap_index in range(3):
        combined = jnp.zeros((frame_count,) + source.shape[1:], source.dtype)
        for which_clip in range(2):
            offset_val = direction * (tap_index - 1) * dilation[which_clip]
            target_ok, target_clip = slot_tables(frame_ids + offset_val, clip_frames)
            keep_mask = usable & target_ok & (clip_ids == which_clip) & (target_clip == which_clip)
            start_row = (out_first + offset_val - first_frame).astype(jnp.int32)
            shifted = lax.dynamic_slice_in_dim(source, start_row, frame_count, 0)
            combined = jnp.where(keep_mask[:, None, None], shifted, combined)
        results.append(combined)
    return results

def time_forward(act_src, first_frame, out_first, frame_count, clip_frames, dilation, temporal):
    pieces = shifted_pieces(act_src, first_frame, out_first, frame_count, clip_frames, dilation, 1)
    summed = jnp.zeros(pieces[0].shape, jnp.float32)
    for tap_index in range(3):
        summed = summed + jnp.dot(pieces[tap_index], temporal[tap_index], preferred_element_type=jnp.float32)
    return summed.astype(jnp.bfloat16)

def time_backward(act_src, grad_src, first_frame, out_first, frame_count, clip_frames, dilation, temporal):
    pieces_act = shifted_pieces(act_src, first_frame, out_first, frame_count, clip_frames, dilation, 1)
    pieces_grad = shifted_pieces(grad_src, first_frame, out_first, frame_count, clip_frames, dilation, -1)
    channels = grad_src.shape[-1]
    own_grad = lax.dynamic_slice_in_dim(grad_src, out_first - first_frame, frame_count, 0)
    flat_grad = own_grad.reshape(-1, channels)
    back_sum = jnp.zeros(pieces_grad[0].shape, jnp.float32)
    weight_terms = []
    for tap_index in range(3):
        back_sum = back_sum + lax.dot_general(pieces_grad[tap_index], temporal[tap_index], (((2,), (1,)), ((), ())), preferred_element_type=jnp.float32)
        weight_terms.append(lax.dot_general(pieces_act[tap_index].reshape(-1, channels), flat_grad, (((0,), (0,)), ((), ())), preferred_element_type=jnp.float32))
    return (back_sum.astype(jnp.bfloat16), jnp.stack(weight_terms))

def widen(padded):
    return jnp.pad(padded, ((0, 0), (0, 0), (1, 1), (0, 0)))

def spatial_forward(padded, spatial):
    row_count = padded.shape[1] - 2
    col_count = padded.shape[2]
    wide = widen(padded)
    summed = jnp.zeros((padded.shape[0], row_count, col_count, spatial.shape[3]), jnp.float32)
    for offset_row in range(3):
        for offset_col in range(3):
            window = wide[:, offset_row:offset_row + row_count, offset_col:offset_col + col_count, :]
            summed = summed + jnp.dot(window, spatial[offset_row, offset_col], preferred_element_type=jnp.float32)
    return summed

def spatial_backward(padded, spatial):
    row_count = padded.shape[1] - 2
    col_count = padded.shape[2]
    wide = widen(padded)
    summed = jnp.zeros((padded.shape[0], row_count, col_count, spatial.shape[2]), jnp.float32)
    for offset_row in range(3):
        for offset_col in range(3):
            window = wide[:, 2 - offset_row:2 - offset_row + row_count, 2 - offset_col:2 - offset_col + col_count, :]
            summed = summed + lax.dot_general(window, spatial[offset_row, offset_col], (((3,), (1,)), ((), ())), preferred_element_type=jnp.float32)
    return summed

def weight_grad(padded, grad_conv):
    row_count = padded.shape[1] - 2
    col_count = padded.shape[2]
    channels = grad_conv.shape[-1]
    wide = widen(padded)
    flat_grad = grad_conv.reshape(-1, channels)
    outer_rows = []
    for offset_row in range(3):
        inner_cols = []
        for offset_col in range(3):
            window = wide[:, offset_row:offset_row + row_count, offset_col:offset_col + col_count, :]
            inner_cols.append(lax.dot_general(window.reshape(-1, window.shape[-1]), flat_grad, (((0,), (0,)), ((), ())), preferred_element_type=jnp.float32))
        outer_rows.append(jnp.stack(inner_cols))
    return jnp.stack(outer_rows)

def group_fold(values):
    return values.reshape(values.shape[0], GROUPS, -1).sum(axis=2)

def spread_groups(values, group_size):
    return jnp.repeat(values, group_size, axis=-1)[:, None, None, :]

def normalize(conv_out, sum_first, sum_second, norm_gain, norm_shift, entries):
    group_size = conv_out.shape[-1] // GROUPS
    mean_val = sum_first / entries
    variance = sum_second / entries - mean_val * mean_val
    inv_std = lax.rsqrt(variance + NORM_EPS)
    inv_wide = spread_groups(inv_std, group_size)
    normed = (conv_out - spread_groups(mean_val, group_size)) * inv_wide
    shaped = normed * norm_gain + norm_shift
    return (normed, shaped, inv_wide)

def gradient_normed(grad_act, shaped, norm_gain):
    sigmoid_val = jax.nn.sigmoid(shaped)
    return grad_act.astype(jnp.float32) * sigmoid_val * (1.0 + shaped * (1.0 - sigmoid_val)) * norm_gain

def norm_backward(grad_normed, normed, inv_wide, mean_first, mean_second):
    group_size = grad_normed.shape[-1] // GROUPS
    result = inv_wide * (grad_normed - spread_groups(mean_first, group_size) - normed * spread_groups(mean_second, group_size))
    return result.astype(jnp.bfloat16)

def reference(frames_in, cotangent, spatial, temporal, norm_gain, norm_shift, clip_frames, dilation):
    slot_count, height, col_count, channels = frames_in.shape
    entries = height * col_count * (channels // GROUPS)
    row_pad = ((0, 0), (1, 1), (0, 0), (0, 0))

    def frame_norm(frame):
        padded = jnp.pad(frame[None], row_pad)
        conv_out = spatial_forward(padded, spatial)
        sums_first = group_fold(lax.optimization_barrier(jnp.sum(conv_out, axis=(1, 2))))
        sums_second = group_fold(lax.optimization_barrier(jnp.sum(conv_out * conv_out, axis=(1, 2))))
        normed, shaped, inv_wide = normalize(conv_out, sums_first, sums_second, norm_gain, norm_shift, entries)
        return (padded, normed, shaped, inv_wide)

    def front(frame):
        padded, normed, shaped, inv_wide = frame_norm(frame)
        return jax.nn.silu(shaped)[0].astype(jnp.bfloat16)
    silu_frames = lax.map(front, frames_in)
    usable, clip_ids = slot_tables(jnp.arange(slot_count, dtype=jnp.int32), clip_frames)
    activation = jnp.where(usable[:, None, None, None], silu_frames, jnp.zeros_like(silu_frames))
    activation = activation.reshape(slot_count, height * col_count, channels)
    grad_rows = cotangent.reshape(slot_count, height * col_count, channels)
    pad_spec = ((DMAX, DMAX), (0, 0), (0, 0))
    act_src = jnp.pad(activation, pad_spec)
    grad_src = jnp.pad(grad_rows, pad_spec)
    temporal_out = time_forward(act_src, -DMAX, 0, slot_count, clip_frames, dilation, temporal)
    grad_act, temporal_grad = time_backward(act_src, grad_src, -DMAX, 0, slot_count, clip_frames, dilation, temporal)
    out_frames = (frames_in.astype(jnp.float32) + temporal_out.reshape(frames_in.shape).astype(jnp.float32)).astype(jnp.bfloat16)
    grad_act = grad_act.reshape(frames_in.shape)

    def back(carry, items):
        frame, grad_frame, cot_frame = items
        padded, normed, shaped, inv_wide = frame_norm(frame)
        grad_normed = gradient_normed(grad_frame[None], shaped, norm_gain)
        mean_first = group_fold(lax.optimization_barrier(jnp.sum(grad_normed, axis=(1, 2)))) / entries
        mean_second = group_fold(lax.optimization_barrier(jnp.sum(grad_normed * normed, axis=(1, 2)))) / entries
        grad_conv = norm_backward(grad_normed, normed, inv_wide, mean_first, mean_second)
        conv_pad = jnp.pad(grad_conv, row_pad)
        in_frame = (cot_frame[None].astype(jnp.float32) + spatial_backward(conv_pad, spatial)).astype(jnp.bfloat16)
        return (carry + weight_grad(padded, grad_conv), in_frame[0])
    spatial_grad, in_grad = lax.scan(back, jnp.zeros(spatial.shape, jnp.float32), (frames_in, grad_act, cotangent))
    return (out_frames, in_grad, spatial_grad, temporal_grad)
```

```python
import functools

import jax
import jax.numpy as jnp
from jax import lax
from jax.experimental import pallas as pl
from jax.experimental.pallas import tpu as pltpu
from jax.sharding import PartitionSpec as P

MESH = pl.DeviceIdType.MESH
F32 = jnp.float32
BF16 = jnp.bfloat16
C = 256
FS = 8
ROWS = 4
COLS = 64
NX = 4
NY = 4
NTM = 32
NZ = 8
LINE = FS * COLS
ENTRIES = float(ROWS * NZ * COLS * 8)
EPS = 1e-05
MID = pl.ds(C, C)


def dot(a, b):
    return jnp.dot(a, b, preferred_element_type=F32)


def fold8(v):
    lane = lax.broadcasted_iota(jnp.int32, v.shape, 1)
    for step in (1, 2, 4):
        low = pltpu.roll(v, C - step, 1)
        high = pltpu.roll(v, step, 1)
        v = v + jnp.where((lane & step) == 0, low, high)
    return v


def shifted(v):
    n = v.shape[0]
    col = lax.broadcasted_iota(jnp.int32, v.shape, 0) & (COLS - 1)
    before = jnp.where(col == 0, 0.0, pltpu.roll(v, 1, 0))
    after = jnp.where(col == COLS - 1, 0.0, pltpu.roll(v, n - 1, 0))
    return before, after


def kernel(
    fr, ct, w_in, t_in, gain_ref, shift_ref, cf, dl,
    tout, ig_out, ag_out,
    xs3, xt, convf, dh, gn, a24, c24, pieces, at, gs3, w3, wt3, t3, tt3,
    st_loc, st_recv, st_fin, wg, s1h, r1, s1, s1c, r2, s2, s2c, r3, zf, zrecv, zag, agb, outv,
    lsem, bsend, brecv, ssend, srecv, rsend, rrecv,
):
    tm = lax.axis_index("tm")
    sp = lax.axis_index("space")
    core = lax.rem(tm, 2)
    yi = lax.rem(lax.div(tm, 2), NY)
    xi = lax.div(tm, 2 * NY)
    pair = tm + 1 - 2 * core
    tm_next = lax.rem(tm + 1, NTM)
    tm_prev = lax.rem(tm + NTM - 1, NTM)
    sp_next = lax.rem(sp + 1, NZ)
    sp_prev = lax.rem(sp + NZ - 1, NZ)

    def at_x(o):
        return (lax.rem(xi + o, NX) * NY + yi) * 2 + core

    def at_y(o):
        return (xi * NY + lax.rem(yi + o, NY)) * 2 + core

    def remote(src, dst, send, recv, device):
        copy = pltpu.make_async_remote_copy(
            src_ref=src, dst_ref=dst, send_sem=send, recv_sem=recv, device_id=device, device_id_type=MESH
        )
        copy.start()
        return copy

    loads = [
        pltpu.make_async_copy(fr.at[:, r], xs3.at[r + 1, :, :, MID], lsem.at[r]) for r in range(ROWS)
    ]
    loads.append(pltpu.make_async_copy(w_in, w3, lsem.at[4]))
    loads.append(pltpu.make_async_copy(t_in, t3, lsem.at[5]))
    loads.append(pltpu.make_async_copy(ct, c24.at[pl.ds(FS, FS)], lsem.at[6]))
    for load in loads:
        load.start()

    far = tm + (2 * core - 1)
    far = lax.rem(far + NTM, NTM)
    partners = [(pair, sp), (far, sp)]
    partners += [(tm, lax.rem(sp + o, NZ)) for o in range(1, NZ)]
    partners += [(at_x(o), sp) for o in range(1, NX)]
    partners += [(at_y(o), sp) for o in range(1, NY)]
    barrier = pltpu.get_barrier_semaphore()
    for partner in partners:
        pl.semaphore_signal(barrier, inc=1, device_id=partner, device_id_type=MESH)
    pl.semaphore_wait(barrier, len(partners))

    sends = []
    halo_x = [
        remote(fr.at[:, ROWS - 1], xs3.at[0, :, :, MID], bsend.at[0], brecv.at[0], (tm, sp_next)),
        remote(fr.at[:, 0], xs3.at[ROWS + 1, :, :, MID], bsend.at[1], brecv.at[1], (tm, sp_prev)),
    ]
    halo_c = [
        remote(ct, c24.at[pl.ds(0, FS)], bsend.at[2], brecv.at[2], (tm_next, sp)),
        remote(ct, c24.at[pl.ds(2 * FS, FS)], bsend.at[3], brecv.at[3], (tm_prev, sp)),
    ]
    sends += halo_x + halo_c

    def widen_row(ref, line, order, keep):
        v = ref[line, :, :, MID].reshape(LINE, C).astype(F32)
        if keep is not None:
            v = v * keep
            ref[line, :, :, MID] = v.astype(BF16).reshape(FS, COLS, C)
        before, after = shifted(v)
        if order < 0:
            before, after = after, before
        ref[line, :, :, pl.ds(0, C)] = before.astype(BF16).reshape(FS, COLS, C)
        ref[line, :, :, pl.ds(2 * C, C)] = after.astype(BF16).reshape(FS, COLS, C)

    def loop(lo, hi, body):
        def step(i, carry):
            body(i)
            return carry

        lax.fori_loop(lo, hi, step, 0)

    for r in range(ROWS):
        loads[r].wait()
    loop(1, ROWS + 1, lambda line: widen_row(xs3, line, 1, None))

    def conv_row(r):
        acc = dot(xs3[r].reshape(LINE, 3 * C), w3[0])
        acc = acc + dot(xs3[r + 1].reshape(LINE, 3 * C), w3[1])
        acc = acc + dot(xs3[r + 2].reshape(LINE, 3 * C), w3[2])
        acc = acc.reshape(FS, COLS, C)
        convf[r] = acc
        st_loc[0, pl.ds(0, FS)] += jnp.sum(acc, axis=1)
        st_loc[0, pl.ds(FS, FS)] += jnp.sum(acc * acc, axis=1)

    st_loc[0] = jnp.zeros((2 * FS, C), F32)
    loads[4].wait()
    loop(1, ROWS - 1, conv_row)

    def transpose_line(line):
        x = xs3[line, :, :, MID].reshape(LINE, C)
        xt[:, pl.ds(pl.multiple_of(line * LINE, LINE), LINE)] = x.T

    loop(1, ROWS + 1, transpose_line)

    def transpose_w(i):
        for j in range(3):
            wt3[i, pl.ds(j * C, C), :] = w3[i, pl.ds(j * C, C), :].T

    loop(0, 3, transpose_w)
    loads[5].wait()
    for k in range(3):
        tt3[pl.ds(k * C, C), :] = t3[pl.ds(k * C, C), :].T

    not_first = (sp > 0).astype(F32)
    not_last = (sp < NZ - 1).astype(F32)
    halo_x[0].wait_recv()
    widen_row(xs3, 0, 1, not_first)
    halo_x[1].wait_recv()
    widen_row(xs3, ROWS + 1, 1, not_last)
    loop(0, 2, lambda t: conv_row(t * (ROWS - 1)))

    def exchange_stats(phase):
        copies = []
        for o in range(1, NZ):
            n = phase * (NZ - 1) + o - 1
            copies.append(
                remote(
                    st_loc.at[phase], st_recv.at[phase, o - 1], ssend.at[n], srecv.at[n],
                    (tm, lax.rem(sp + o, NZ)),
                )
            )
        return copies

    def total_stats(phase, copies):
        total = st_loc[phase]
        for o in range(1, NZ):
            copies[o - 1].wait_recv()
            total = total + st_recv[phase, o - 1]
        return fold8(total) * (1.0 / ENTRIES)

    stats = exchange_stats(0)
    sends += stats
    loop(0, 2, lambda t: transpose_line(t * (ROWS + 1)))
    total = total_stats(0, stats)
    mean = total[0:FS]
    variance = total[FS : 2 * FS] - mean * mean
    st_fin[0] = mean
    st_fin[1] = lax.rsqrt(variance + EPS)

    first = cf[0]
    filled = cf[0] + cf[1]
    gain = gain_ref[...]
    bias = shift_ref[...]

    def activate(f):
        frame = tm * FS + f
        used = (frame < filled).astype(F32)
        v = convf[:, f].reshape(ROWS * COLS, C)
        normed = (v - st_fin[0, pl.ds(f, 1)]) * st_fin[1, pl.ds(f, 1)]
        shaped = normed * gain + bias
        sig = 0.5 * jnp.tanh(0.5 * shaped) + 0.5
        act = shaped * sig * used
        a24[FS + f] = act.astype(BF16).reshape(ROWS, COLS, C)
        convf[:, f] = normed.reshape(ROWS, COLS, C)
        dh[:, f] = (sig * (1.0 + shaped * (1.0 - sig)) * gain).reshape(ROWS, COLS, C)

    loop(0, FS, activate)
    own = pl.ds(FS, FS)
    halo_a = [
        remote(a24.at[own], a24.at[pl.ds(0, FS)], bsend.at[4], brecv.at[4], (tm_next, sp)),
        remote(a24.at[own], a24.at[pl.ds(2 * FS, FS)], bsend.at[5], brecv.at[5], (tm_prev, sp)),
    ]
    sends += halo_a

    def gather(source, f, direction):
        frame = tm * FS + f
        second = (frame >= first).astype(jnp.int32)
        gap = jnp.where(second == 1, dl[1], dl[0])
        for k in range(3):
            move = direction * (k - 1) * gap
            target = frame + move
            same = (target >= first).astype(jnp.int32) == second
            live = (frame < filled) & (target >= 0) & (target < filled) & same
            slot = jnp.clip(FS + f + move, 0, 3 * FS - 1)
            v = source[slot].astype(F32) * live.astype(F32)
            pieces[f, :, :, pl.ds(k * C, C)] = v.astype(BF16)

    loads[6].wait()
    for copy in halo_c:
        copy.wait_recv()

    def backward_time(f):
        gather(c24, f, -1)
        back = dot(pieces[f].reshape(ROWS * COLS, 3 * C), tt3[...]).astype(BF16).astype(F32)
        grad = back * dh[:, f].reshape(ROWS * COLS, C)
        gn[:, f] = grad.reshape(ROWS, COLS, C)
        normed = convf[:, f].reshape(ROWS * COLS, C)
        st_loc[1, pl.ds(f, 1)] = jnp.sum(grad, axis=0, keepdims=True)
        st_loc[1, pl.ds(FS + f, 1)] = jnp.sum(grad * normed, axis=0, keepdims=True)

    loop(0, FS, backward_time)
    stats = exchange_stats(1)
    sends += stats

    first_axis = [(at_y, yi), (at_x, xi), (at_y, yi), (at_x, xi)]
    second_axis = [(at_x, xi), (at_y, yi), (at_x, xi), (at_y, yi)]
    half = C // 2
    stage1 = [None] * 4
    stage2 = [None] * 4
    stage3 = [None] * 4

    def begin1(b):
        other = pl.ds(pl.multiple_of((1 - core) * half, half), half)
        s1h[b] = wg[b, other, :].astype(BF16)
        stage1[b] = remote(s1h.at[b], r1.at[b], rsend.at[b, 0], rrecv.at[b, 0], (pair, sp))
        sends.append(stage1[b])

    def begin2(b):
        stage1[b].wait_recv()
        mine = pl.ds(pl.multiple_of(core * half, half), half)
        v = wg[b, mine, :] + r1[b].astype(F32)
        s1[b] = v
        s1c[b] = v.astype(BF16)
        place, index = first_axis[b]
        stage2[b] = []
        for o in range(1, 4):
            rows = pl.ds(pl.multiple_of(lax.rem(index + o, 4) * 32, 32), 32)
            stage2[b].append(
                remote(
                    s1c.at[b, rows, :], r2.at[b, o - 1], rsend.at[b, o], rrecv.at[b, o], (place(o), sp)
                )
            )
        sends.extend(stage2[b])

    def begin3(b):
        index = first_axis[b][1]
        v = s1[b, pl.ds(pl.multiple_of(index * 32, 32), 32), :]
        for o in range(1, 4):
            stage2[b][o - 1].wait_recv()
            v = v + r2[b, o - 1].astype(F32)
        for q in range(4):
            part = v[(q // 2) * 16 : (q // 2) * 16 + 16, (q % 2) * 384 : (q % 2) * 384 + 384]
            s2[b, q] = part
            s2c[b, q] = part.astype(BF16)
        place, index = second_axis[b]
        stage3[b] = []
        for o in range(1, 4):
            stage3[b].append(
                remote(
                    s2c.at[b, lax.rem(index + o, 4)], r3.at[b, o - 1], rsend.at[b, 3 + o],
                    rrecv.at[b, 3 + o], (place(o), sp),
                )
            )
        sends.extend(stage3[b])

    def finish3(b):
        v = s2[b, second_axis[b][1]]
        for o in range(1, 4):
            stage3[b][o - 1].wait_recv()
            v = v + r3[b, o - 1].astype(F32)
        zf[pl.ds(2 * b, 2)] = v.reshape(2, 8, 384)

    def transpose_act(f):
        x = a24[FS + f].reshape(ROWS * COLS, C)
        at[:, pl.ds(pl.multiple_of(f * ROWS * COLS, ROWS * COLS), ROWS * COLS)] = x.T

    loop(0, FS, transpose_act)
    wg[0] = dot(at[...], pieces[...].reshape(FS * ROWS * COLS, 3 * C))
    begin1(0)

    total = total_stats(1, stats)
    st_fin[2] = total[0:FS]
    st_fin[3] = total[FS : 2 * FS]

    def conv_grad(r, f):
        v = st_fin[1, pl.ds(f, 1)] * (
            gn[r, f] - st_fin[2, pl.ds(f, 1)] - convf[r, f] * st_fin[3, pl.ds(f, 1)]
        )
        v16 = v.astype(BF16)
        before, after = shifted(v16.astype(F32))
        gs3[r + 1, f, :, pl.ds(0, C)] = after.astype(BF16)
        gs3[r + 1, f, :, MID] = v16
        gs3[r + 1, f, :, pl.ds(2 * C, C)] = before.astype(BF16)

    def conv_grad_edges(f):
        conv_grad(0, f)
        conv_grad(ROWS - 1, f)

    def conv_grad_inner(f):
        conv_grad(1, f)
        conv_grad(2, f)

    loop(0, FS, conv_grad_edges)
    halo_g = [
        remote(gs3.at[ROWS, :, :, MID], gs3.at[0, :, :, MID], bsend.at[6], brecv.at[6], (tm, sp_next)),
        remote(gs3.at[1, :, :, MID], gs3.at[ROWS + 1, :, :, MID], bsend.at[7], brecv.at[7], (tm, sp_prev)),
    ]
    sends += halo_g
    loop(0, FS, conv_grad_inner)
    begin2(0)

    for i in range(3):
        wg[i + 1] = dot(
            xt[:, pl.ds(i * LINE, ROWS * LINE)], gs3[pl.ds(1, ROWS)].reshape(ROWS * LINE, 3 * C)
        )
        begin1(i + 1)
    begin3(0)
    for b in (1, 2, 3):
        begin2(b)

    def in_row(r):
        acc = dot(gs3[r + 2].reshape(LINE, 3 * C), wt3[0])
        acc = acc + dot(gs3[r + 1].reshape(LINE, 3 * C), wt3[1])
        acc = acc + dot(gs3[r].reshape(LINE, 3 * C), wt3[2])
        acc = acc.reshape(FS, COLS, C) + c24[pl.ds(FS, FS), r].astype(F32)
        outv[0, :, r] = acc.astype(BF16)

    loop(1, ROWS - 1, in_row)
    for b in (1, 2, 3):
        begin3(b)
    halo_g[0].wait_recv()
    widen_row(gs3, 0, -1, not_first)
    halo_g[1].wait_recv()
    widen_row(gs3, ROWS + 1, -1, not_last)
    for b in range(4):
        finish3(b)
    z1 = []
    for o in range(1, NZ):
        q = lax.rem(sp + o, NZ)
        z1.append(remote(zf.at[q], zrecv.at[o - 1], ssend.at[13 + o], srecv.at[13 + o], (tm, q)))
    sends += z1
    loop(0, 2, lambda t: in_row(t * (ROWS - 1)))
    out_ig = pltpu.make_async_copy(outv.at[0], ig_out, lsem.at[7])
    out_ig.start()

    v = zf[sp]
    for o in range(1, NZ):
        z1[o - 1].wait_recv()
        v = v + zrecv[o - 1]
    zag[sp] = v
    z2 = []
    for o in range(1, NZ):
        q = lax.rem(sp + o, NZ)
        z2.append(remote(zag.at[sp], zag.at[sp], ssend.at[20 + o], srecv.at[20 + o], (tm, q)))
    sends += z2

    for copy in halo_a:
        copy.wait_recv()

    def forward_time(f):
        gather(a24, f, 1)
        outv[1, f] = (
            dot(pieces[f].reshape(ROWS * COLS, 3 * C), t3[...]).astype(BF16).reshape(ROWS, COLS, C)
        )

    loop(0, FS, forward_time)
    out_t = pltpu.make_async_copy(outv.at[1], tout, lsem.at[8])
    out_t.start()

    for copy in z2:
        copy.wait_recv()
    g3 = []
    for b in range(4):
        n1, n2 = first_axis[b][1], second_axis[b][1]
        agb[b, core, n1, n2] = zag[pl.ds(2 * b, 2)].reshape(16, 384).astype(BF16)
        place = second_axis[b][0]
        here = agb.at[b, core, n1, n2]
        g3.append(
            [remote(here, here, rsend.at[b, 6 + o], rrecv.at[b, 6 + o], (place(o), sp)) for o in range(1, 4)]
        )
        sends += g3[b]
    g2 = []
    for b in range(4):
        for copy in g3[b]:
            copy.wait_recv()
        place, n1 = first_axis[b]
        here = agb.at[b, core, n1]
        g2.append(
            [remote(here, here, rsend.at[b, 9 + o], rrecv.at[b, 9 + o], (place(o), sp)) for o in range(1, 4)]
        )
        sends += g2[b]
    g1 = []
    for b in range(4):
        for copy in g2[b]:
            copy.wait_recv()
        here = agb.at[b, core]
        g1.append(remote(here, here, rsend.at[b, 13], rrecv.at[b, 13], (pair, sp)))
    sends += g1
    out_g = []
    for b in range(4):
        g1[b].wait_recv()
        out_g.append(pltpu.make_async_copy(agb.at[b], ag_out.at[b], lsem.at[9 + b]))
        out_g[b].start()
    for copy in sends:
        copy.wait_send()
    out_ig.wait()
    out_t.wait()
    for copy in out_g:
        copy.wait()


def section(frames_in, cotangent, spatial, temporal, norm_gain, norm_shift, clip_frames, dilation):
    any_spec = pl.BlockSpec(memory_space=pl.ANY)
    vmem_spec = pl.BlockSpec(memory_space=pltpu.VMEM)
    smem_spec = pl.BlockSpec(memory_space=pltpu.SMEM)
    shape = (FS, ROWS, COLS, C)
    V = pltpu.VMEM
    DMA = pltpu.SemaphoreType.DMA
    tout, ig, ag = pl.pallas_call(
        kernel,
        out_shape=(
            jax.ShapeDtypeStruct(shape, BF16),
            jax.ShapeDtypeStruct(shape, BF16),
            jax.ShapeDtypeStruct((4, 2, 4, 4, 16, 384), BF16),
        ),
        in_specs=[any_spec] * 4 + [vmem_spec] * 2 + [smem_spec] * 2,
        out_specs=(any_spec, any_spec, any_spec),
        scratch_shapes=[
            V((ROWS + 2, FS, COLS, 3 * C), BF16),
            V((C, (ROWS + 2) * LINE), BF16),
            V((ROWS, FS, COLS, C), F32),
            V((ROWS, FS, COLS, C), F32),
            V((ROWS, FS, COLS, C), F32),
            V((3 * FS, ROWS, COLS, C), BF16),
            V((3 * FS, ROWS, COLS, C), BF16),
            V((FS, ROWS, COLS, 3 * C), BF16),
            V((C, FS * ROWS * COLS), BF16),
            V((ROWS + 2, FS, COLS, 3 * C), BF16),
            V((3, 3 * C, C), BF16),
            V((3, 3 * C, C), BF16),
            V((3 * C, C), BF16),
            V((3 * C, C), BF16),
            V((2, 2 * FS, C), F32),
            V((2, NZ - 1, 2 * FS, C), F32),
            V((4, FS, C), F32),
            V((4, C, 3 * C), F32),
            V((4, C // 2, 3 * C), BF16),
            V((4, C // 2, 3 * C), BF16),
            V((4, C // 2, 3 * C), F32),
            V((4, C // 2, 3 * C), BF16),
            V((4, 3, 32, 3 * C), BF16),
            V((4, 4, 16, 384), F32),
            V((4, 4, 16, 384), BF16),
            V((4, 3, 16, 384), BF16),
            V((NZ, 8, 384), F32),
            V((NZ - 1, 8, 384), F32),
            V((NZ, 8, 384), F32),
            V((4, 2, 4, 4, 16, 384), BF16),
            V((2,) + shape, BF16),
            DMA((13,)),
            DMA((8,)),
            DMA((8,)),
            DMA((28,)),
            DMA((28,)),
            DMA((4, 14)),
            DMA((4, 14)),
        ],
        compiler_params=pltpu.CompilerParams(
            collective_id=0, has_side_effects=True, vmem_limit_bytes=58 * 1024 * 1024
        ),
        cost_estimate=pl.CostEstimate(flops=9_700_000_000, bytes_accessed=9_000_000, transcendentals=0),
    )(
        frames_in,
        cotangent,
        spatial.reshape(3, 3 * C, C),
        temporal.reshape(3 * C, C),
        norm_gain.reshape(1, C),
        norm_shift.reshape(1, C),
        clip_frames,
        dilation,
    )
    out_frames = (frames_in.astype(F32) + tout.astype(F32)).astype(BF16)
    grads = ag.reshape(4, 8, 2, 2, 16, 384).transpose(0, 1, 2, 4, 3, 5).reshape(4, C, 3, C)
    grads = grads.transpose(0, 2, 1, 3).astype(F32)
    return out_frames, ig, grads[1:], grads[0]


def solution(mesh):
    frames = P("tm", "space", None, None)
    return jax.shard_map(
        section,
        mesh=mesh,
        in_specs=(frames, frames, P(), P(), P(), P(), P(), P()),
        out_specs=(frames, frames, P(), P()),
        check_vma=False,
    )
```

```python
import functools

import jax
import jax.numpy as jnp
from jax import lax
from jax.experimental import pallas as pl
from jax.experimental.pallas import tpu as pltpu
from jax.sharding import PartitionSpec as P

MESH = pl.DeviceIdType.MESH
F32 = jnp.float32
BF16 = jnp.bfloat16
C = 256
FS = 8
ROWS = 4
COLS = 64
NX = 4
NY = 4
NTM = 32
NZ = 8
LINE = FS * COLS
ENTRIES = float(ROWS * NZ * COLS * 8)
EPS = 1e-05
MID = pl.ds(C, C)


def dot(a, b):
    return jnp.dot(a, b, preferred_element_type=F32)


def fold8(v):
    lane = lax.broadcasted_iota(jnp.int32, v.shape, 1)
    for step in (1, 2, 4):
        low = pltpu.roll(v, C - step, 1)
        high = pltpu.roll(v, step, 1)
        v = v + jnp.where((lane & step) == 0, low, high)
    return v


def shifted(v):
    n = v.shape[0]
    col = lax.broadcasted_iota(jnp.int32, v.shape, 0) & (COLS - 1)
    before = jnp.where(col == 0, 0.0, pltpu.roll(v, 1, 0))
    after = jnp.where(col == COLS - 1, 0.0, pltpu.roll(v, n - 1, 0))
    return before, after


def kernel(
    fr, ct, w_in, t_in, gain_ref, shift_ref, cf, dl,
    tout, ig_out, ag_out,
    xs3, xt, convf, dh, gn, a24, c24, pieces, at, gs3, w3, wt3, t3, tt3,
    st_loc, st_recv, st_fin, wg, s1h, r1, s1, s1c, r2, s2, s2c, r3, zf, zrecv, zag, agb, outv,
    lsem, osem, bsend, brecv, ssend, srecv, rsend, rrecv,
):
    tm = lax.axis_index("tm")
    sp = lax.axis_index("space")
    core = lax.rem(tm, 2)
    yi = lax.rem(lax.div(tm, 2), NY)
    xi = lax.div(tm, 2 * NY)
    pair = tm + 1 - 2 * core
    tm_next = lax.rem(tm + 1, NTM)
    tm_prev = lax.rem(tm + NTM - 1, NTM)
    sp_next = lax.rem(sp + 1, NZ)
    sp_prev = lax.rem(sp + NZ - 1, NZ)

    def at_x(o):
        return (lax.rem(xi + o, NX) * NY + yi) * 2 + core

    def at_y(o):
        return (xi * NY + lax.rem(yi + o, NY)) * 2 + core

    def remote(src, dst, send, recv, device):
        copy = pltpu.make_async_remote_copy(
            src_ref=src, dst_ref=dst, send_sem=send, recv_sem=recv, device_id=device, device_id_type=MESH
        )
        copy.start()
        return copy

    loads = [
        pltpu.make_async_copy(fr.at[:, r], xs3.at[r + 1, :, :, MID], lsem.at[r]) for r in range(ROWS)
    ]
    loads.append(pltpu.make_async_copy(w_in, w3, lsem.at[4]))
    loads.append(pltpu.make_async_copy(t_in, t3, lsem.at[5]))
    loads.append(pltpu.make_async_copy(ct, c24.at[pl.ds(FS, FS)], lsem.at[6]))
    for load in loads:
        load.start()

    far = tm + (2 * core - 1)
    far = lax.rem(far + NTM, NTM)
    partners = [(pair, sp), (far, sp)]
    partners += [(tm, lax.rem(sp + o, NZ)) for o in range(1, NZ)]
    partners += [(at_x(o), sp) for o in range(1, NX)]
    partners += [(at_y(o), sp) for o in range(1, NY)]
    barrier = pltpu.get_barrier_semaphore()
    for partner in partners:
        pl.semaphore_signal(barrier, inc=1, device_id=partner, device_id_type=MESH)
    pl.semaphore_wait(barrier, len(partners))

    sends = []
    halo_x = [
        remote(fr.at[:, ROWS - 1], xs3.at[0, :, :, MID], bsend.at[0], brecv.at[0], (tm, sp_next)),
        remote(fr.at[:, 0], xs3.at[ROWS + 1, :, :, MID], bsend.at[1], brecv.at[1], (tm, sp_prev)),
    ]
    halo_c = [
        remote(ct, c24.at[pl.ds(0, FS)], bsend.at[2], brecv.at[2], (tm_next, sp)),
        remote(ct, c24.at[pl.ds(2 * FS, FS)], bsend.at[3], brecv.at[3], (tm_prev, sp)),
    ]
    sends += halo_x + halo_c

    def widen_row(ref, line, order, keep):
        v = ref[line, :, :, MID].reshape(LINE, C).astype(F32)
        if keep is not None:
            v = v * keep
            ref[line, :, :, MID] = v.astype(BF16).reshape(FS, COLS, C)
        before, after = shifted(v)
        if order < 0:
            before, after = after, before
        ref[line, :, :, pl.ds(0, C)] = before.astype(BF16).reshape(FS, COLS, C)
        ref[line, :, :, pl.ds(2 * C, C)] = after.astype(BF16).reshape(FS, COLS, C)

    def loop(lo, hi, body):
        def step(i, carry):
            body(i)
            return carry

        lax.fori_loop(lo, hi, step, 0)

    for r in range(ROWS):
        loads[r].wait()
    loop(1, ROWS + 1, lambda line: widen_row(xs3, line, 1, None))

    def conv_row(r):
        acc = dot(xs3[r].reshape(LINE, 3 * C), w3[0])
        acc = acc + dot(xs3[r + 1].reshape(LINE, 3 * C), w3[1])
        acc = acc + dot(xs3[r + 2].reshape(LINE, 3 * C), w3[2])
        acc = acc.reshape(FS, COLS, C)
        convf[r] = acc
        st_loc[0, pl.ds(0, FS)] += jnp.sum(acc, axis=1)
        st_loc[0, pl.ds(FS, FS)] += jnp.sum(acc * acc, axis=1)

    st_loc[0] = jnp.zeros((2 * FS, C), F32)
    loads[4].wait()
    loop(1, ROWS - 1, conv_row)

    def edge_start(t):
        line = 1 + t * (ROWS - 2)
        acc = dot(xs3[line].reshape(LINE, 3 * C), w3[1 - t])
        acc = acc + dot(xs3[line + 1].reshape(LINE, 3 * C), w3[2 - t])
        convf[t * (ROWS - 1)] = acc.reshape(FS, COLS, C)

    def edge_finish(t):
        r = t * (ROWS - 1)
        acc = dot(xs3[t * (ROWS + 1)].reshape(LINE, 3 * C), w3[2 * t])
        acc = acc.reshape(FS, COLS, C) + convf[r]
        convf[r] = acc
        st_loc[0, pl.ds(0, FS)] += jnp.sum(acc, axis=1)
        st_loc[0, pl.ds(FS, FS)] += jnp.sum(acc * acc, axis=1)

    loop(0, 2, edge_start)

    def transpose_line(line):
        x = xs3[line, :, :, MID].reshape(LINE, C)
        xt[:, pl.ds(pl.multiple_of(line * LINE, LINE), LINE)] = x.T

    loop(1, ROWS + 1, transpose_line)

    def transpose_w(i):
        for j in range(3):
            wt3[i, pl.ds(j * C, C), :] = w3[i, pl.ds(j * C, C), :].T

    loop(0, 3, transpose_w)
    loads[5].wait()
    for k in range(3):
        tt3[pl.ds(k * C, C), :] = t3[pl.ds(k * C, C), :].T

    not_first = (sp > 0).astype(F32)
    not_last = (sp < NZ - 1).astype(F32)
    halo_x[0].wait_recv()
    widen_row(xs3, 0, 1, not_first)
    halo_x[1].wait_recv()
    widen_row(xs3, ROWS + 1, 1, not_last)
    loop(0, 2, edge_finish)

    def exchange_stats(phase):
        copies = []
        for o in range(1, NZ):
            n = phase * (NZ - 1) + o - 1
            copies.append(
                remote(
                    st_loc.at[phase], st_recv.at[phase, o - 1], ssend.at[n], srecv.at[n],
                    (tm, lax.rem(sp + o, NZ)),
                )
            )
        return copies

    def total_stats(phase, copies):
        total = st_loc[phase]
        for o in range(1, NZ):
            copies[o - 1].wait_recv()
            total = total + st_recv[phase, o - 1]
        return fold8(total) * (1.0 / ENTRIES)

    stats = exchange_stats(0)
    sends += stats
    loop(0, 2, lambda t: transpose_line(t * (ROWS + 1)))
    total = total_stats(0, stats)
    mean = total[0:FS]
    variance = total[FS : 2 * FS] - mean * mean
    st_fin[0] = mean
    st_fin[1] = lax.rsqrt(variance + EPS)

    first = cf[0]
    filled = cf[0] + cf[1]
    gain = gain_ref[...]
    bias = shift_ref[...]

    def activate(f):
        frame = tm * FS + f
        used = (frame < filled).astype(F32)
        v = convf[:, f].reshape(ROWS * COLS, C)
        normed = (v - st_fin[0, pl.ds(f, 1)]) * st_fin[1, pl.ds(f, 1)]
        shaped = normed * gain + bias
        sig = 0.5 * jnp.tanh(0.5 * shaped) + 0.5
        act = shaped * sig * used
        a24[FS + f] = act.astype(BF16).reshape(ROWS, COLS, C)
        convf[:, f] = normed.reshape(ROWS, COLS, C)
        dh[:, f] = (sig * (1.0 + shaped * (1.0 - sig)) * gain).reshape(ROWS, COLS, C)

    loop(0, FS, activate)
    own = pl.ds(FS, FS)
    halo_a = [
        remote(a24.at[own], a24.at[pl.ds(0, FS)], bsend.at[4], brecv.at[4], (tm_next, sp)),
        remote(a24.at[own], a24.at[pl.ds(2 * FS, FS)], bsend.at[5], brecv.at[5], (tm_prev, sp)),
    ]
    sends += halo_a

    def gather(source, f, direction, taps):
        frame = tm * FS + f
        second = (frame >= first).astype(jnp.int32)
        gap = jnp.where(second == 1, dl[1], dl[0])
        for k in taps:
            move = direction * (k - 1) * gap
            target = frame + move
            same = (target >= first).astype(jnp.int32) == second
            live = (frame < filled) & (target >= 0) & (target < filled) & same
            slot = jnp.clip(FS + f + move, 0, 3 * FS - 1)
            keep = jnp.full((ROWS, COLS, C), live.astype(F32)).astype(BF16)
            pieces[f, :, :, pl.ds(k * C, C)] = source[slot] * keep

    loads[6].wait()
    loop(0, FS, lambda f: gather(c24, f, -1, (1,)))
    for copy in halo_c:
        copy.wait_recv()

    def backward_time(f):
        gather(c24, f, -1, (0, 2))
        back = dot(pieces[f].reshape(ROWS * COLS, 3 * C), tt3[...]).astype(BF16).astype(F32)
        grad = back * dh[:, f].reshape(ROWS * COLS, C)
        gn[:, f] = grad.reshape(ROWS, COLS, C)
        normed = convf[:, f].reshape(ROWS * COLS, C)
        st_loc[1, pl.ds(f, 1)] = jnp.sum(grad, axis=0, keepdims=True)
        st_loc[1, pl.ds(FS + f, 1)] = jnp.sum(grad * normed, axis=0, keepdims=True)

    loop(0, FS, backward_time)
    stats = exchange_stats(1)
    sends += stats

    first_axis = [(at_y, yi), (at_x, xi), (at_x, xi), (at_y, yi)]
    second_axis = [(at_x, xi), (at_y, yi), (at_y, yi), (at_x, xi)]
    half = C // 2
    stage1 = [None] * 4
    stage2 = [None] * 4
    stage3 = [None] * 4

    def begin1(b):
        other = pl.ds(pl.multiple_of((1 - core) * half, half), half)
        s1h[b] = wg[b, other, :].astype(BF16)
        stage1[b] = remote(s1h.at[b], r1.at[b], rsend.at[b, 0], rrecv.at[b, 0], (pair, sp))
        sends.append(stage1[b])

    def begin2(b):
        stage1[b].wait_recv()
        mine = pl.ds(pl.multiple_of(core * half, half), half)
        v = wg[b, mine, :] + r1[b].astype(F32)
        s1[b] = v
        s1c[b] = v.astype(BF16)
        place, index = first_axis[b]
        stage2[b] = []
        for o in range(1, 4):
            rows = pl.ds(pl.multiple_of(lax.rem(index + o, 4) * 32, 32), 32)
            stage2[b].append(
                remote(
                    s1c.at[b, rows, :], r2.at[b, o - 1], rsend.at[b, o], rrecv.at[b, o], (place(o), sp)
                )
            )
        sends.extend(stage2[b])

    def begin3(b):
        index = first_axis[b][1]
        v = s1[b, pl.ds(pl.multiple_of(index * 32, 32), 32), :]
        for o in range(1, 4):
            stage2[b][o - 1].wait_recv()
            v = v + r2[b, o - 1].astype(F32)
        for q in range(4):
            part = v[(q // 2) * 16 : (q // 2) * 16 + 16, (q % 2) * 384 : (q % 2) * 384 + 384]
            s2[b, q] = part
            s2c[b, q] = part.astype(BF16)
        place, index = second_axis[b]
        stage3[b] = []
        for o in range(1, 4):
            stage3[b].append(
                remote(
                    s2c.at[b, lax.rem(index + o, 4)], r3.at[b, o - 1], rsend.at[b, 3 + o],
                    rrecv.at[b, 3 + o], (place(o), sp),
                )
            )
        sends.extend(stage3[b])

    def finish3(b):
        v = s2[b, second_axis[b][1]]
        for o in range(1, 4):
            stage3[b][o - 1].wait_recv()
            v = v + r3[b, o - 1].astype(F32)
        zf[pl.ds(2 * b, 2)] = v.reshape(2, 8, 384)

    def transpose_act(f):
        x = a24[FS + f].reshape(ROWS * COLS, C)
        at[:, pl.ds(pl.multiple_of(f * ROWS * COLS, ROWS * COLS), ROWS * COLS)] = x.T

    loop(0, FS, transpose_act)
    wg[0] = dot(at[...], pieces[...].reshape(FS * ROWS * COLS, 3 * C))
    begin1(0)

    total = total_stats(1, stats)
    st_fin[2] = total[0:FS]
    st_fin[3] = total[FS : 2 * FS]

    def conv_grad(r, f):
        v = st_fin[1, pl.ds(f, 1)] * (
            gn[r, f] - st_fin[2, pl.ds(f, 1)] - convf[r, f] * st_fin[3, pl.ds(f, 1)]
        )
        v16 = v.astype(BF16)
        before, after = shifted(v16.astype(F32))
        gs3[r + 1, f, :, pl.ds(0, C)] = after.astype(BF16)
        gs3[r + 1, f, :, MID] = v16
        gs3[r + 1, f, :, pl.ds(2 * C, C)] = before.astype(BF16)

    def conv_grad_edges(f):
        conv_grad(0, f)
        conv_grad(ROWS - 1, f)

    def conv_grad_inner(f):
        conv_grad(1, f)
        conv_grad(2, f)

    loop(0, FS, conv_grad_edges)
    halo_g = [
        remote(gs3.at[ROWS, :, :, MID], gs3.at[0, :, :, MID], bsend.at[6], brecv.at[6], (tm, sp_next)),
        remote(gs3.at[1, :, :, MID], gs3.at[ROWS + 1, :, :, MID], bsend.at[7], brecv.at[7], (tm, sp_prev)),
    ]
    sends += halo_g
    loop(0, FS, conv_grad_inner)
    begin2(0)

    for i in range(3):
        wg[i + 1] = dot(
            xt[:, pl.ds(i * LINE, ROWS * LINE)], gs3[pl.ds(1, ROWS)].reshape(ROWS * LINE, 3 * C)
        )
        begin1(i + 1)
        if i > 0:
            begin2(i)
    begin2(3)
    begin3(0)

    def in_row(r):
        acc = dot(gs3[r + 2].reshape(LINE, 3 * C), wt3[0])
        acc = acc + dot(gs3[r + 1].reshape(LINE, 3 * C), wt3[1])
        acc = acc + dot(gs3[r].reshape(LINE, 3 * C), wt3[2])
        acc = acc.reshape(FS, COLS, C) + c24[pl.ds(FS, FS), r].astype(F32)
        outv[0, :, r] = acc.astype(BF16)

    loop(1, ROWS - 1, in_row)
    for b in (1, 2, 3):
        begin3(b)
    halo_g[0].wait_recv()
    widen_row(gs3, 0, -1, not_first)
    halo_g[1].wait_recv()
    widen_row(gs3, ROWS + 1, -1, not_last)
    for b in range(4):
        finish3(b)
    z1 = []
    for o in range(1, NZ):
        q = lax.rem(sp + o, NZ)
        z1.append(remote(zf.at[q], zrecv.at[o - 1], ssend.at[13 + o], srecv.at[13 + o], (tm, q)))
    sends += z1
    loop(0, 2, lambda t: in_row(t * (ROWS - 1)))
    out_ig = pltpu.make_async_copy(outv.at[0], ig_out, lsem.at[7])
    out_ig.start()

    v = zf[sp]
    for o in range(1, NZ):
        z1[o - 1].wait_recv()
        v = v + zrecv[o - 1]
    zag[sp] = v
    z2 = []
    for o in range(1, NZ):
        q = lax.rem(sp + o, NZ)
        z2.append(remote(zag.at[sp], zag.at[sp], ssend.at[20 + o], srecv.at[20 + o], (tm, q)))
    sends += z2

    for copy in halo_a:
        copy.wait_recv()

    def forward_time(f):
        gather(a24, f, 1, (0, 1, 2))
        moved = dot(pieces[f].reshape(ROWS * COLS, 3 * C), t3[...]).astype(BF16).astype(F32)
        x = xs3[pl.ds(1, ROWS), f, :, MID].astype(F32)
        outv[1, f] = (x + moved.reshape(ROWS, COLS, C)).astype(BF16)

    loop(0, FS, forward_time)
    out_t = pltpu.make_async_copy(outv.at[1], tout, lsem.at[8])
    out_t.start()

    for copy in z2:
        copy.wait_recv()
    g3 = []
    for b in range(4):
        n1, n2 = first_axis[b][1], second_axis[b][1]
        agb[b, core, n1, n2] = zag[pl.ds(2 * b, 2)].reshape(16, 384).astype(BF16)
        place = second_axis[b][0]
        here = agb.at[b, core, n1, n2]
        g3.append(
            [remote(here, here, rsend.at[b, 6 + o], rrecv.at[b, 6 + o], (place(o), sp)) for o in range(1, 4)]
        )
        sends += g3[b]
    g2 = []
    for b in range(4):
        for copy in g3[b]:
            copy.wait_recv()
        place, n1 = first_axis[b]
        here = agb.at[b, core, n1]
        g2.append(
            [remote(here, here, rsend.at[b, 9 + o], rrecv.at[b, 9 + o], (place(o), sp)) for o in range(1, 4)]
        )
        sends += g2[b]
    g1 = []
    out_g = []
    for b in range(4):
        n1 = first_axis[b][1]
        for o in range(4):
            if o > 0:
                g2[b][o - 1].wait_recv()
            here = lax.rem(n1 + 4 - o, 4)
            g1.append(
                remote(
                    agb.at[b, core, here], ag_out.at[b, core, here], rsend.at[b, 13 + o],
                    rrecv.at[b, 13 + o], (pair, sp),
                )
            )
            out_g.append(
                pltpu.make_async_copy(agb.at[b, core, here], ag_out.at[b, core, here], osem.at[b, o])
            )
            out_g[-1].start()
    sends += g1
    for copy in g1:
        copy.wait_recv()
    for copy in sends:
        copy.wait_send()
    out_ig.wait()
    out_t.wait()
    for copy in out_g:
        copy.wait()


def deliver(of_in, ig_in, ag, of, ig, sg, tg, agv, full, frames, csem, gsem):
    loads = [pltpu.make_async_copy(ag.at[b], agv.at[b], gsem.at[b]) for b in range(4)]
    for load in loads:
        load.start()
    quarter = FS // 4
    parts = []
    for n in range(4):
        part = pl.ds(n * quarter, quarter)
        parts.append((of_in.at[part], frames.at[0, part], of.at[part], csem.at[0, n]))
        parts.append((ig_in.at[part], frames.at[1, part], ig.at[part], csem.at[1, n]))
    arrivals = [pltpu.make_async_copy(source, stage, sem) for source, stage, _, sem in parts]
    for copy in arrivals:
        copy.start()
    copies = []
    for copy, (_, stage, target, sem) in zip(arrivals, parts):
        copy.wait()
        copies.append(pltpu.make_async_copy(stage, target, sem))
        copies[-1].start()
    stores = []
    for b in range(4):
        loads[b].wait()

        def place(m, carry):
            for q in range(4):
                rows = pl.ds(pl.multiple_of(m * 32 + (q // 2) * 16, 16), 16)
                v = agv[b, lax.div(m, 4), lax.rem(m, 4), q].astype(F32)
                if q % 2 == 0:
                    full[3 * b, rows, :] = v[:, 0:C]
                    full[3 * b + 1, rows, pl.ds(0, 128)] = v[:, C:384]
                else:
                    full[3 * b + 1, rows, pl.ds(128, 128)] = v[:, 0:128]
                    full[3 * b + 2, rows, :] = v[:, 128:384]
            return carry

        lax.fori_loop(0, 8, place, 0)
        target = tg if b == 0 else sg.at[pl.ds(3 * (b - 1), 3)]
        stores.append(pltpu.make_async_copy(full.at[pl.ds(3 * b, 3)], target, gsem.at[b]))
        stores[b].start()
    for copy in copies + stores:
        copy.wait()


def section(frames_in, cotangent, spatial, temporal, norm_gain, norm_shift, clip_frames, dilation):
    any_spec = pl.BlockSpec(memory_space=pl.ANY)
    vmem_spec = pl.BlockSpec(memory_space=pltpu.VMEM)
    smem_spec = pl.BlockSpec(memory_space=pltpu.SMEM)
    shape = (FS, ROWS, COLS, C)
    V = pltpu.VMEM
    DMA = pltpu.SemaphoreType.DMA
    tout, ig, ag = pl.pallas_call(
        kernel,
        out_shape=(
            jax.ShapeDtypeStruct(shape, BF16),
            jax.ShapeDtypeStruct(shape, BF16),
            jax.ShapeDtypeStruct((4, 2, 4, 4, 16, 384), BF16),
        ),
        in_specs=[any_spec] * 4 + [vmem_spec] * 2 + [smem_spec] * 2,
        out_specs=(any_spec, any_spec, any_spec),
        scratch_shapes=[
            V((ROWS + 2, FS, COLS, 3 * C), BF16),
            V((C, (ROWS + 2) * LINE), BF16),
            V((ROWS, FS, COLS, C), F32),
            V((ROWS, FS, COLS, C), F32),
            V((ROWS, FS, COLS, C), F32),
            V((3 * FS, ROWS, COLS, C), BF16),
            V((3 * FS, ROWS, COLS, C), BF16),
            V((FS, ROWS, COLS, 3 * C), BF16),
            V((C, FS * ROWS * COLS), BF16),
            V((ROWS + 2, FS, COLS, 3 * C), BF16),
            V((3, 3 * C, C), BF16),
            V((3, 3 * C, C), BF16),
            V((3 * C, C), BF16),
            V((3 * C, C), BF16),
            V((2, 2 * FS, C), F32),
            V((2, NZ - 1, 2 * FS, C), F32),
            V((4, FS, C), F32),
            V((4, C, 3 * C), F32),
            V((4, C // 2, 3 * C), BF16),
            V((4, C // 2, 3 * C), BF16),
            V((4, C // 2, 3 * C), F32),
            V((4, C // 2, 3 * C), BF16),
            V((4, 3, 32, 3 * C), BF16),
            V((4, 4, 16, 384), F32),
            V((4, 4, 16, 384), BF16),
            V((4, 3, 16, 384), BF16),
            V((NZ, 8, 384), F32),
            V((NZ - 1, 8, 384), F32),
            V((NZ, 8, 384), F32),
            V((4, 2, 4, 4, 16, 384), BF16),
            V((2,) + shape, BF16),
            DMA((9,)),
            DMA((4, 4)),
            DMA((8,)),
            DMA((8,)),
            DMA((28,)),
            DMA((28,)),
            DMA((4, 17)),
            DMA((4, 17)),
        ],
        compiler_params=pltpu.CompilerParams(
            collective_id=0, has_side_effects=True, vmem_limit_bytes=58 * 1024 * 1024
        ),
        cost_estimate=pl.CostEstimate(flops=9_700_000_000, bytes_accessed=9_000_000, transcendentals=0),
    )(
        frames_in,
        cotangent,
        spatial.reshape(3, 3 * C, C),
        temporal.reshape(3 * C, C),
        norm_gain.reshape(1, C),
        norm_shift.reshape(1, C),
        clip_frames,
        dilation,
    )
    out_frames, in_grad, spatial_grad, temporal_grad = pl.pallas_call(
        deliver,
        out_shape=(
            jax.ShapeDtypeStruct(shape, BF16),
            jax.ShapeDtypeStruct(shape, BF16),
            jax.ShapeDtypeStruct((9, C, C), F32),
            jax.ShapeDtypeStruct((3, C, C), F32),
        ),
        in_specs=[any_spec] * 3,
        out_specs=(any_spec,) * 4,
        scratch_shapes=[V((4, 2, 4, 4, 16, 384), BF16), V((12, C, C), F32), V((2,) + shape, BF16), DMA((2, 4)), DMA((4,))],
        compiler_params=pltpu.CompilerParams(vmem_limit_bytes=58 * 1024 * 1024),
        cost_estimate=pl.CostEstimate(flops=0, bytes_accessed=9_000_000, transcendentals=0),
    )(tout, ig, ag)
    return out_frames, in_grad, spatial_grad.reshape(3, 3, C, C), temporal_grad


def solution(mesh):
    frames = P("tm", "space", None, None)
    return jax.shard_map(
        section,
        mesh=mesh,
        in_specs=(frames, frames, P(), P(), P(), P(), P(), P()),
        out_specs=(frames, frames, P(), P()),
        check_vma=False,
    )
```

```python
import functools

import jax
import jax.numpy as jnp
from jax import lax
from jax.experimental import pallas as pl
from jax.experimental.pallas import tpu as pltpu
from jax.sharding import PartitionSpec as P

MESH = pl.DeviceIdType.MESH
F32 = jnp.float32
BF16 = jnp.bfloat16
C = 256
FS = 8
ROWS = 4
COLS = 64
NX = 4
NY = 4
NTM = 32
NZ = 8
LINE = FS * COLS
ENTRIES = float(ROWS * NZ * COLS * 8)
EPS = 1e-05
MID = pl.ds(C, C)
FAR_FIRST = (4, 3, 5, 2, 6, 1, 7)


def dot(a, b):
    return jnp.dot(a, b, preferred_element_type=F32)


def fold8(v):
    lane = lax.broadcasted_iota(jnp.int32, v.shape, 1)
    for step in (1, 2, 4):
        low = pltpu.roll(v, C - step, 1)
        high = pltpu.roll(v, step, 1)
        v = v + jnp.where((lane & step) == 0, low, high)
    return v


def shifted(v):
    n = v.shape[0]
    col = lax.broadcasted_iota(jnp.int32, v.shape, 0) & (COLS - 1)
    before = jnp.where(col == 0, 0.0, pltpu.roll(v, 1, 0))
    after = jnp.where(col == COLS - 1, 0.0, pltpu.roll(v, n - 1, 0))
    return before, after


def kernel(
    fr, ct, w_in, t_in, gain_in, shift_in, cf_in, dl_in,
    tout, ig_out, ag_out,
    xs3, xt, convf, dh, gn, a24, c24, pieces, at, gs3, w3, wt3, t3, tt3,
    st_loc, st_recv, st_fin, wg, s1h, r1, s1, s1c, r2, s2, s2c, r3, zf, zrecv, zag, agb, outv,
    gain_ref, shift_ref, cf, dl,
    lsem, osem, bsend, brecv, ssend, srecv, rsend, rrecv,
):
    tm = lax.axis_index("tm")
    sp = lax.axis_index("space")
    core = lax.rem(tm, 2)
    yi = lax.rem(lax.div(tm, 2), NY)
    xi = lax.div(tm, 2 * NY)
    pair = tm + 1 - 2 * core
    tm_next = lax.rem(tm + 1, NTM)
    tm_prev = lax.rem(tm + NTM - 1, NTM)
    sp_next = lax.rem(sp + 1, NZ)
    sp_prev = lax.rem(sp + NZ - 1, NZ)

    def at_x(o):
        return (lax.rem(xi + o, NX) * NY + yi) * 2 + core

    def at_y(o):
        return (xi * NY + lax.rem(yi + o, NY)) * 2 + core

    def remote(src, dst, send, recv, device):
        copy = pltpu.make_async_remote_copy(
            src_ref=src, dst_ref=dst, send_sem=send, recv_sem=recv, device_id=device, device_id_type=MESH
        )
        copy.start()
        return copy

    far = tm + (2 * core - 1)
    far = lax.rem(far + NTM, NTM)
    partners = [(pair, sp), (far, sp)]
    partners += [(tm, lax.rem(sp + o, NZ)) for o in range(1, NZ)]
    partners += [(at_x(o), sp) for o in range(1, NX)]
    partners += [(at_y(o), sp) for o in range(1, NY)]
    barrier = pltpu.get_barrier_semaphore()
    for partner in partners:
        pl.semaphore_signal(barrier, inc=1, device_id=partner, device_id_type=MESH)
    loads = [
        pltpu.make_async_copy(fr.at[:, r], xs3.at[r + 1, :, :, MID], lsem.at[r]) for r in range(ROWS)
    ]
    loads.append(pltpu.make_async_copy(w_in, w3, lsem.at[4]))
    loads.append(pltpu.make_async_copy(t_in, t3, lsem.at[5]))
    loads.append(pltpu.make_async_copy(ct, c24.at[pl.ds(FS, FS)], lsem.at[6]))
    small = [(gain_in, gain_ref), (shift_in, shift_ref), (cf_in, cf), (dl_in, dl)]
    loads += [pltpu.make_async_copy(source, target, lsem.at[9 + n]) for n, (source, target) in enumerate(small)]
    for load in loads:
        load.start()

    pl.semaphore_wait(barrier, len(partners))

    sends = []
    halo_x = [
        remote(fr.at[:, ROWS - 1], xs3.at[0, :, :, MID], bsend.at[0], brecv.at[0], (tm, sp_next)),
        remote(fr.at[:, 0], xs3.at[ROWS + 1, :, :, MID], bsend.at[1], brecv.at[1], (tm, sp_prev)),
    ]
    halo_c = [
        remote(ct, c24.at[pl.ds(0, FS)], bsend.at[2], brecv.at[2], (tm_next, sp)),
        remote(ct, c24.at[pl.ds(2 * FS, FS)], bsend.at[3], brecv.at[3], (tm_prev, sp)),
    ]
    sends += halo_x + halo_c

    def widen_row(ref, line, order, keep):
        v = ref[line, :, :, MID].reshape(LINE, C).astype(F32)
        if keep is not None:
            v = v * keep
            ref[line, :, :, MID] = v.astype(BF16).reshape(FS, COLS, C)
        before, after = shifted(v)
        if order < 0:
            before, after = after, before
        ref[line, :, :, pl.ds(0, C)] = before.astype(BF16).reshape(FS, COLS, C)
        ref[line, :, :, pl.ds(2 * C, C)] = after.astype(BF16).reshape(FS, COLS, C)

    def loop(lo, hi, body):
        def step(i, carry):
            body(i)
            return carry

        lax.fori_loop(lo, hi, step, 0)

    for r in range(ROWS):
        loads[r].wait()
    loop(1, ROWS + 1, lambda line: widen_row(xs3, line, 1, None))

    def conv_row(r):
        acc = dot(xs3[r].reshape(LINE, 3 * C), w3[0])
        acc = acc + dot(xs3[r + 1].reshape(LINE, 3 * C), w3[1])
        acc = acc + dot(xs3[r + 2].reshape(LINE, 3 * C), w3[2])
        acc = acc.reshape(FS, COLS, C)
        convf[r] = acc
        st_loc[0, pl.ds(0, FS)] += jnp.sum(acc, axis=1)
        st_loc[0, pl.ds(FS, FS)] += jnp.sum(acc * acc, axis=1)

    st_loc[0] = jnp.zeros((2 * FS, C), F32)
    loads[4].wait()
    loop(1, ROWS - 1, conv_row)

    def edge_start(t):
        line = 1 + t * (ROWS - 2)
        acc = dot(xs3[line].reshape(LINE, 3 * C), w3[1 - t])
        acc = acc + dot(xs3[line + 1].reshape(LINE, 3 * C), w3[2 - t])
        convf[t * (ROWS - 1)] = acc.reshape(FS, COLS, C)

    def edge_finish(t):
        r = t * (ROWS - 1)
        acc = dot(xs3[t * (ROWS + 1)].reshape(LINE, 3 * C), w3[2 * t])
        acc = acc.reshape(FS, COLS, C) + convf[r]
        convf[r] = acc
        st_loc[0, pl.ds(0, FS)] += jnp.sum(acc, axis=1)
        st_loc[0, pl.ds(FS, FS)] += jnp.sum(acc * acc, axis=1)

    loop(0, 2, edge_start)

    def transpose_line(line):
        x = xs3[line, :, :, MID].reshape(LINE, C)
        xt[:, pl.ds(pl.multiple_of(line * LINE, LINE), LINE)] = x.T

    loop(1, ROWS + 1, transpose_line)

    def transpose_w(i):
        for j in range(3):
            wt3[i, pl.ds(j * C, C), :] = w3[i, pl.ds(j * C, C), :].T

    loop(0, 3, transpose_w)
    loads[5].wait()
    for k in range(3):
        tt3[pl.ds(k * C, C), :] = t3[pl.ds(k * C, C), :].T

    not_first = (sp > 0).astype(F32)
    not_last = (sp < NZ - 1).astype(F32)
    halo_x[0].wait_recv()
    widen_row(xs3, 0, 1, not_first)
    halo_x[1].wait_recv()
    widen_row(xs3, ROWS + 1, 1, not_last)
    loop(0, 2, edge_finish)

    def exchange_stats(phase):
        copies = {}
        for o in FAR_FIRST:
            n = phase * (NZ - 1) + o - 1
            copies[o] = remote(
                st_loc.at[phase], st_recv.at[phase, o - 1], ssend.at[n], srecv.at[n],
                (tm, lax.rem(sp + o, NZ)),
            )
        sends.extend(copies.values())
        return copies

    def total_stats(phase, copies):
        total = st_loc[phase]
        for o in range(1, NZ):
            copies[o].wait_recv()
            total = total + st_recv[phase, o - 1]
        return fold8(total) * (1.0 / ENTRIES)

    stats = exchange_stats(0)
    loop(0, 2, lambda t: transpose_line(t * (ROWS + 1)))
    total = total_stats(0, stats)
    mean = total[0:FS]
    variance = total[FS : 2 * FS] - mean * mean
    st_fin[0] = mean
    st_fin[1] = lax.rsqrt(variance + EPS)

    for load in loads[7:]:
        load.wait()
    first = cf[0]
    filled = cf[0] + cf[1]
    gain = gain_ref[...]
    bias = shift_ref[...]

    def activate(f):
        frame = tm * FS + f
        used = (frame < filled).astype(F32)
        v = convf[:, f].reshape(ROWS * COLS, C)
        normed = (v - st_fin[0, pl.ds(f, 1)]) * st_fin[1, pl.ds(f, 1)]
        shaped = normed * gain + bias
        sig = 0.5 * jnp.tanh(0.5 * shaped) + 0.5
        act = shaped * sig * used
        a24[FS + f] = act.astype(BF16).reshape(ROWS, COLS, C)
        convf[:, f] = normed.reshape(ROWS, COLS, C)
        dh[:, f] = (sig * (1.0 + shaped * (1.0 - sig)) * gain).reshape(ROWS, COLS, C)

    loop(0, FS, activate)
    own = pl.ds(FS, FS)
    halo_a = [
        remote(a24.at[own], a24.at[pl.ds(0, FS)], bsend.at[4], brecv.at[4], (tm_next, sp)),
        remote(a24.at[own], a24.at[pl.ds(2 * FS, FS)], bsend.at[5], brecv.at[5], (tm_prev, sp)),
    ]
    sends += halo_a

    def gather(source, f, direction, taps):
        frame = tm * FS + f
        second = (frame >= first).astype(jnp.int32)
        gap = jnp.where(second == 1, dl[1], dl[0])
        for k in taps:
            move = direction * (k - 1) * gap
            target = frame + move
            same = (target >= first).astype(jnp.int32) == second
            live = (frame < filled) & (target >= 0) & (target < filled) & same
            slot = jnp.clip(FS + f + move, 0, 3 * FS - 1)
            keep = jnp.full((ROWS, COLS, C), live.astype(F32)).astype(BF16)
            pieces[f, :, :, pl.ds(k * C, C)] = source[slot] * keep

    loads[6].wait()
    loop(0, FS, lambda f: gather(c24, f, -1, (1,)))
    for copy in halo_c:
        copy.wait_recv()

    def backward_time(f):
        gather(c24, f, -1, (0, 2))
        back = dot(pieces[f].reshape(ROWS * COLS, 3 * C), tt3[...]).astype(BF16).astype(F32)
        grad = back * dh[:, f].reshape(ROWS * COLS, C)
        gn[:, f] = grad.reshape(ROWS, COLS, C)
        normed = convf[:, f].reshape(ROWS * COLS, C)
        st_loc[1, pl.ds(f, 1)] = jnp.sum(grad, axis=0, keepdims=True)
        st_loc[1, pl.ds(FS + f, 1)] = jnp.sum(grad * normed, axis=0, keepdims=True)

    loop(0, FS, backward_time)
    stats = exchange_stats(1)

    first_axis = [(at_y, yi), (at_x, xi), (at_x, xi), (at_y, yi)]
    second_axis = [(at_x, xi), (at_y, yi), (at_y, yi), (at_x, xi)]
    half = C // 2
    stage1 = [None] * 4
    stage2 = [None] * 4
    stage3 = [None] * 4

    def begin1(b):
        other = pl.ds(pl.multiple_of((1 - core) * half, half), half)
        s1h[b] = wg[b, other, :].astype(BF16)
        stage1[b] = remote(s1h.at[b], r1.at[b], rsend.at[b, 0], rrecv.at[b, 0], (pair, sp))
        sends.append(stage1[b])

    def begin2(b):
        stage1[b].wait_recv()
        mine = pl.ds(pl.multiple_of(core * half, half), half)
        v = wg[b, mine, :] + r1[b].astype(F32)
        s1[b] = v
        s1c[b] = v.astype(BF16)
        place, index = first_axis[b]
        stage2[b] = []
        for o in range(1, 4):
            rows = pl.ds(pl.multiple_of(lax.rem(index + o, 4) * 32, 32), 32)
            stage2[b].append(
                remote(
                    s1c.at[b, rows, :], r2.at[b, o - 1], rsend.at[b, o], rrecv.at[b, o], (place(o), sp)
                )
            )
        sends.extend(stage2[b])

    def begin3(b):
        index = first_axis[b][1]
        v = s1[b, pl.ds(pl.multiple_of(index * 32, 32), 32), :]
        for o in range(1, 4):
            stage2[b][o - 1].wait_recv()
            v = v + r2[b, o - 1].astype(F32)
        for q in range(4):
            part = v[(q // 2) * 16 : (q // 2) * 16 + 16, (q % 2) * 384 : (q % 2) * 384 + 384]
            s2[b, q] = part
            s2c[b, q] = part.astype(BF16)
        place, index = second_axis[b]
        stage3[b] = []
        for o in range(1, 4):
            stage3[b].append(
                remote(
                    s2c.at[b, lax.rem(index + o, 4)], r3.at[b, o - 1], rsend.at[b, 3 + o],
                    rrecv.at[b, 3 + o], (place(o), sp),
                )
            )
        sends.extend(stage3[b])

    def finish3(b):
        v = s2[b, second_axis[b][1]]
        for o in range(1, 4):
            stage3[b][o - 1].wait_recv()
            v = v + r3[b, o - 1].astype(F32)
        zf[pl.ds(2 * b, 2)] = v.reshape(2, 8, 384)

    def transpose_act(f):
        x = a24[FS + f].reshape(ROWS * COLS, C)
        at[:, pl.ds(pl.multiple_of(f * ROWS * COLS, ROWS * COLS), ROWS * COLS)] = x.T

    loop(0, FS, transpose_act)
    wg[0] = dot(at[...], pieces[...].reshape(FS * ROWS * COLS, 3 * C))
    begin1(0)

    total = total_stats(1, stats)
    st_fin[2] = total[0:FS]
    st_fin[3] = total[FS : 2 * FS]

    def conv_grad(r, f):
        v = st_fin[1, pl.ds(f, 1)] * (
            gn[r, f] - st_fin[2, pl.ds(f, 1)] - convf[r, f] * st_fin[3, pl.ds(f, 1)]
        )
        v16 = v.astype(BF16)
        before, after = shifted(v16.astype(F32))
        gs3[r + 1, f, :, pl.ds(0, C)] = after.astype(BF16)
        gs3[r + 1, f, :, MID] = v16
        gs3[r + 1, f, :, pl.ds(2 * C, C)] = before.astype(BF16)

    def conv_grad_edges(f):
        conv_grad(0, f)
        conv_grad(ROWS - 1, f)

    def conv_grad_inner(f):
        conv_grad(1, f)
        conv_grad(2, f)

    loop(0, FS, conv_grad_edges)
    halo_g = [
        remote(gs3.at[ROWS, :, :, MID], gs3.at[0, :, :, MID], bsend.at[6], brecv.at[6], (tm, sp_next)),
        remote(gs3.at[1, :, :, MID], gs3.at[ROWS + 1, :, :, MID], bsend.at[7], brecv.at[7], (tm, sp_prev)),
    ]
    sends += halo_g
    loop(0, FS, conv_grad_inner)
    begin2(0)

    for i in range(3):
        wg[i + 1] = dot(
            xt[:, pl.ds(i * LINE, ROWS * LINE)], gs3[pl.ds(1, ROWS)].reshape(ROWS * LINE, 3 * C)
        )
        begin1(i + 1)
        if i > 0:
            begin2(i)
    begin2(3)
    begin3(0)

    def in_row(r):
        acc = dot(gs3[r + 2].reshape(LINE, 3 * C), wt3[0])
        acc = acc + dot(gs3[r + 1].reshape(LINE, 3 * C), wt3[1])
        acc = acc + dot(gs3[r].reshape(LINE, 3 * C), wt3[2])
        acc = acc.reshape(FS, COLS, C) + c24[pl.ds(FS, FS), r].astype(F32)
        outv[0, :, r] = acc.astype(BF16)

    loop(1, ROWS - 1, in_row)
    for b in (1, 2, 3):
        begin3(b)
    halo_g[0].wait_recv()
    widen_row(gs3, 0, -1, not_first)
    halo_g[1].wait_recv()
    widen_row(gs3, ROWS + 1, -1, not_last)
    for b in range(4):
        finish3(b)
    z1 = {}
    for o in FAR_FIRST:
        q = lax.rem(sp + o, NZ)
        z1[o] = (remote(zf.at[q], zrecv.at[o - 1], ssend.at[13 + o], srecv.at[13 + o], (tm, q)))
    sends += z1.values()
    loop(0, 2, lambda t: in_row(t * (ROWS - 1)))
    out_ig = pltpu.make_async_copy(outv.at[0], ig_out, lsem.at[7])
    out_ig.start()

    v = zf[sp]
    for o in range(1, NZ):
        z1[o].wait_recv()
        v = v + zrecv[o - 1]
    zag[sp] = v
    z2 = []
    for o in FAR_FIRST:
        q = lax.rem(sp + o, NZ)
        z2.append(remote(zag.at[sp], zag.at[sp], ssend.at[20 + o], srecv.at[20 + o], (tm, q)))
    sends += z2

    for copy in halo_a:
        copy.wait_recv()

    def forward_time(f):
        gather(a24, f, 1, (0, 1, 2))
        moved = dot(pieces[f].reshape(ROWS * COLS, 3 * C), t3[...]).astype(BF16).astype(F32)
        x = xs3[pl.ds(1, ROWS), f, :, MID].astype(F32)
        outv[1, f] = (x + moved.reshape(ROWS, COLS, C)).astype(BF16)

    loop(0, FS, forward_time)
    out_t = pltpu.make_async_copy(outv.at[1], tout, lsem.at[8])
    out_t.start()

    for copy in z2:
        copy.wait_recv()
    g3 = []
    for b in range(4):
        n1, n2 = first_axis[b][1], second_axis[b][1]
        agb[b, core, n1, n2] = zag[pl.ds(2 * b, 2)].reshape(16, 384).astype(BF16)
        place = second_axis[b][0]
        here = agb.at[b, core, n1, n2]
        g3.append(
            [remote(here, here, rsend.at[b, 6 + o], rrecv.at[b, 6 + o], (place(o), sp)) for o in (2, 1, 3)]
        )
        sends += g3[b]
    g2 = [{} for _ in range(4)]
    for c in (0, 1, 3, 2):
        for b in range(4):
            if c > 0:
                g3[b][(2, 1, 3).index(c)].wait_recv()
            place, n1 = first_axis[b]
            here = agb.at[b, core, n1, lax.rem(second_axis[b][1] + 4 - c, 4)]
            for o in (2, 1, 3):
                n = 6 + 4 * o + c
                g2[b][o, c] = remote(here, here, rsend.at[b, n], rrecv.at[b, n], (place(o), sp))
            sends += [g2[b][o, c] for o in (2, 1, 3)]
    g1 = []
    out_g = []
    for o in (0, 1, 3, 2):
        for b in range(4):
            if o > 0:
                for c in (0, 1, 3, 2):
                    g2[b][o, c].wait_recv()
            here = lax.rem(first_axis[b][1] + 4 - o, 4)
            g1.append(
                remote(
                    agb.at[b, core, here], ag_out.at[b, core, here], rsend.at[b, 22 + o],
                    rrecv.at[b, 22 + o], (pair, sp),
                )
            )
            out_g.append(
                pltpu.make_async_copy(agb.at[b, core, here], ag_out.at[b, core, here], osem.at[b, o])
            )
            out_g[-1].start()
    sends += g1
    for copy in g1:
        copy.wait_recv()
    for copy in sends:
        copy.wait_send()
    out_ig.wait()
    out_t.wait()
    for copy in out_g:
        copy.wait()


def deliver(of_in, ig_in, ag, of, ig, sg, tg, agv, full, frames, csem, gsem):
    loads = [pltpu.make_async_copy(ag.at[b], agv.at[b], gsem.at[b]) for b in range(4)]
    for load in loads:
        load.start()
    quarter = FS // 4
    parts = []
    for n in range(4):
        part = pl.ds(n * quarter, quarter)
        parts.append((of_in.at[part], frames.at[0, part], of.at[part], csem.at[0, n]))
        parts.append((ig_in.at[part], frames.at[1, part], ig.at[part], csem.at[1, n]))
    arrivals = [pltpu.make_async_copy(source, stage, sem) for source, stage, _, sem in parts]
    for copy in arrivals:
        copy.start()
    stores = []
    for b in range(4):
        loads[b].wait()

        def place(m, carry):
            for q in range(4):
                rows = pl.ds(pl.multiple_of(m * 32 + (q // 2) * 16, 16), 16)
                v = agv[b, lax.div(m, 4), lax.rem(m, 4), q].astype(F32)
                if q % 2 == 0:
                    full[3 * b, rows, :] = v[:, 0:C]
                    full[3 * b + 1, rows, pl.ds(0, 128)] = v[:, C:384]
                else:
                    full[3 * b + 1, rows, pl.ds(128, 128)] = v[:, 0:128]
                    full[3 * b + 2, rows, :] = v[:, 128:384]
            return carry

        lax.fori_loop(0, 8, place, 0)
        target = tg if b == 0 else sg.at[pl.ds(3 * (b - 1), 3)]
        stores.append(pltpu.make_async_copy(full.at[pl.ds(3 * b, 3)], target, gsem.at[b]))
        stores[b].start()
    copies = []
    for copy, (_, stage, target, sem) in zip(arrivals, parts):
        copy.wait()
        copies.append(pltpu.make_async_copy(stage, target, sem))
        copies[-1].start()
    for copy in copies + stores:
        copy.wait()


def section(frames_in, cotangent, spatial, temporal, norm_gain, norm_shift, clip_frames, dilation):
    any_spec = pl.BlockSpec(memory_space=pl.ANY)
    shape = (FS, ROWS, COLS, C)
    V = pltpu.VMEM
    DMA = pltpu.SemaphoreType.DMA
    tout, ig, ag = pl.pallas_call(
        kernel,
        out_shape=(
            jax.ShapeDtypeStruct(shape, BF16),
            jax.ShapeDtypeStruct(shape, BF16),
            jax.ShapeDtypeStruct((4, 2, 4, 4, 16, 384), BF16),
        ),
        in_specs=[any_spec] * 8,
        out_specs=(any_spec, any_spec, any_spec),
        scratch_shapes=[
            V((ROWS + 2, FS, COLS, 3 * C), BF16),
            V((C, (ROWS + 2) * LINE), BF16),
            V((ROWS, FS, COLS, C), F32),
            V((ROWS, FS, COLS, C), F32),
            V((ROWS, FS, COLS, C), F32),
            V((3 * FS, ROWS, COLS, C), BF16),
            V((3 * FS, ROWS, COLS, C), BF16),
            V((FS, ROWS, COLS, 3 * C), BF16),
            V((C, FS * ROWS * COLS), BF16),
            V((ROWS + 2, FS, COLS, 3 * C), BF16),
            V((3, 3 * C, C), BF16),
            V((3, 3 * C, C), BF16),
            V((3 * C, C), BF16),
            V((3 * C, C), BF16),
            V((2, 2 * FS, C), F32),
            V((2, NZ - 1, 2 * FS, C), F32),
            V((4, FS, C), F32),
            V((4, C, 3 * C), F32),
            V((4, C // 2, 3 * C), BF16),
            V((4, C // 2, 3 * C), BF16),
            V((4, C // 2, 3 * C), F32),
            V((4, C // 2, 3 * C), BF16),
            V((4, 3, 32, 3 * C), BF16),
            V((4, 4, 16, 384), F32),
            V((4, 4, 16, 384), BF16),
            V((4, 3, 16, 384), BF16),
            V((NZ, 8, 384), F32),
            V((NZ - 1, 8, 384), F32),
            V((NZ, 8, 384), F32),
            V((4, 2, 4, 4, 16, 384), BF16),
            V((2,) + shape, BF16),
            V((1, C), F32),
            V((1, C), F32),
            pltpu.SMEM((2,), jnp.int32),
            pltpu.SMEM((2,), jnp.int32),
            DMA((13,)),
            DMA((4, 4)),
            DMA((8,)),
            DMA((8,)),
            DMA((28,)),
            DMA((28,)),
            DMA((4, 26)),
            DMA((4, 26)),
        ],
        compiler_params=pltpu.CompilerParams(
            collective_id=0, has_side_effects=True, vmem_limit_bytes=58 * 1024 * 1024
        ),
        cost_estimate=pl.CostEstimate(flops=9_700_000_000, bytes_accessed=9_000_000, transcendentals=0),
    )(
        frames_in,
        cotangent,
        spatial.reshape(3, 3 * C, C),
        temporal.reshape(3 * C, C),
        norm_gain.reshape(1, C),
        norm_shift.reshape(1, C),
        clip_frames,
        dilation,
    )
    out_frames, in_grad, spatial_grad, temporal_grad = pl.pallas_call(
        deliver,
        out_shape=(
            jax.ShapeDtypeStruct(shape, BF16),
            jax.ShapeDtypeStruct(shape, BF16),
            jax.ShapeDtypeStruct((9, C, C), F32),
            jax.ShapeDtypeStruct((3, C, C), F32),
        ),
        in_specs=[any_spec] * 3,
        out_specs=(any_spec,) * 4,
        scratch_shapes=[V((4, 2, 4, 4, 16, 384), BF16), V((12, C, C), F32), V((2,) + shape, BF16), DMA((2, 4)), DMA((4,))],
        compiler_params=pltpu.CompilerParams(vmem_limit_bytes=58 * 1024 * 1024),
        cost_estimate=pl.CostEstimate(flops=0, bytes_accessed=9_000_000, transcendentals=0),
    )(tout, ig, ag)
    return out_frames, in_grad, spatial_grad.reshape(3, 3, C, C), temporal_grad


def solution(mesh):
    frames = P("tm", "space", None, None)
    return jax.shard_map(
        section,
        mesh=mesh,
        in_specs=(frames, frames, P(), P(), P(), P(), P(), P()),
        out_specs=(frames, frames, P(), P()),
        check_vma=False,
    )
```

```python
import functools

import jax
import jax.numpy as jnp
from jax import lax
from jax.experimental import pallas as pl
from jax.experimental.pallas import tpu as pltpu
from jax.sharding import PartitionSpec as P

MESH = pl.DeviceIdType.MESH
F32 = jnp.float32
BF16 = jnp.bfloat16
C = 256
FS = 8
ROWS = 4
COLS = 64
NX = 4
NY = 4
NTM = 32
NZ = 8
LINE = FS * COLS
ENTRIES = float(ROWS * NZ * COLS * 8)
EPS = 1e-05
MID = pl.ds(C, C)
FAR_FIRST = (4, 3, 5, 2, 6, 1, 7)


def dot(a, b):
    return jnp.dot(a, b, preferred_element_type=F32)


def fold8(v):
    lane = lax.broadcasted_iota(jnp.int32, v.shape, 1)
    for step in (1, 2, 4):
        low = pltpu.roll(v, C - step, 1)
        high = pltpu.roll(v, step, 1)
        v = v + jnp.where((lane & step) == 0, low, high)
    return v


def shifted(v):
    n = v.shape[0]
    col = lax.broadcasted_iota(jnp.int32, v.shape, 0) & (COLS - 1)
    before = jnp.where(col == 0, 0.0, pltpu.roll(v, 1, 0))
    after = jnp.where(col == COLS - 1, 0.0, pltpu.roll(v, n - 1, 0))
    return before, after


def kernel(
    fr, ct, w_in, t_in, gain_in, shift_in, cf_in, dl_in,
    tout, ig_out, ag_out,
    xs3, xt, convf, dh, gn, a24, c24, pieces, at, gs3, w3, wt3, t3, tt3,
    st_loc, st_recv, st_fin, wg, s1h, r1, s1, s1c, r2, s2, s2c, r3, zf, zrecv, zag, agb, outv,
    gain_ref, shift_ref, cf, dl,
    lsem, osem, bsend, brecv, ssend, srecv, rsend, rrecv,
):
    tm = lax.axis_index("tm")
    sp = lax.axis_index("space")
    core = lax.rem(tm, 2)
    yi = lax.rem(lax.div(tm, 2), NY)
    xi = lax.div(tm, 2 * NY)
    pair = tm + 1 - 2 * core
    tm_next = lax.rem(tm + 1, NTM)
    tm_prev = lax.rem(tm + NTM - 1, NTM)
    sp_next = lax.rem(sp + 1, NZ)
    sp_prev = lax.rem(sp + NZ - 1, NZ)

    def at_x(o):
        return (lax.rem(xi + o, NX) * NY + yi) * 2 + core

    def at_y(o):
        return (xi * NY + lax.rem(yi + o, NY)) * 2 + core

    def remote(src, dst, send, recv, device):
        copy = pltpu.make_async_remote_copy(
            src_ref=src, dst_ref=dst, send_sem=send, recv_sem=recv, device_id=device, device_id_type=MESH
        )
        copy.start()
        return copy

    far = tm + (2 * core - 1)
    far = lax.rem(far + NTM, NTM)
    partners = [(pair, sp), (far, sp)]
    partners += [(tm, lax.rem(sp + o, NZ)) for o in range(1, NZ)]
    partners += [(at_x(o), sp) for o in range(1, NX)]
    partners += [(at_y(o), sp) for o in range(1, NY)]
    barrier = pltpu.get_barrier_semaphore()
    for partner in partners:
        pl.semaphore_signal(barrier, inc=1, device_id=partner, device_id_type=MESH)
    loads = [
        pltpu.make_async_copy(fr.at[:, r], xs3.at[r + 1, :, :, MID], lsem.at[r]) for r in range(ROWS)
    ]
    loads.append(pltpu.make_async_copy(w_in, w3, lsem.at[4]))
    loads.append(pltpu.make_async_copy(t_in, t3, lsem.at[5]))
    loads.append(pltpu.make_async_copy(ct, c24.at[pl.ds(FS, FS)], lsem.at[6]))
    small = [(gain_in, gain_ref), (shift_in, shift_ref), (cf_in, cf), (dl_in, dl)]
    loads += [pltpu.make_async_copy(source, target, lsem.at[9 + n]) for n, (source, target) in enumerate(small)]
    for load in loads:
        load.start()

    pl.semaphore_wait(barrier, len(partners))

    sends = []
    halo_x = [
        remote(fr.at[:, ROWS - 1], xs3.at[0, :, :, MID], bsend.at[0], brecv.at[0], (tm, sp_next)),
        remote(fr.at[:, 0], xs3.at[ROWS + 1, :, :, MID], bsend.at[1], brecv.at[1], (tm, sp_prev)),
    ]
    halo_c = [
        remote(ct, c24.at[pl.ds(0, FS)], bsend.at[2], brecv.at[2], (tm_next, sp)),
        remote(ct, c24.at[pl.ds(2 * FS, FS)], bsend.at[3], brecv.at[3], (tm_prev, sp)),
    ]
    sends += halo_x + halo_c

    def widen_row(ref, line, order, keep):
        v = ref[line, :, :, MID].reshape(LINE, C).astype(F32)
        if keep is not None:
            v = v * keep
            ref[line, :, :, MID] = v.astype(BF16).reshape(FS, COLS, C)
        before, after = shifted(v)
        if order < 0:
            before, after = after, before
        ref[line, :, :, pl.ds(0, C)] = before.astype(BF16).reshape(FS, COLS, C)
        ref[line, :, :, pl.ds(2 * C, C)] = after.astype(BF16).reshape(FS, COLS, C)

    def loop(lo, hi, body):
        def step(i, carry):
            body(i)
            return carry

        lax.fori_loop(lo, hi, step, 0)

    for r in range(ROWS):
        loads[r].wait()
    loop(1, ROWS + 1, lambda line: widen_row(xs3, line, 1, None))

    def conv_row(r):
        acc = dot(xs3[r].reshape(LINE, 3 * C), w3[0])
        acc = acc + dot(xs3[r + 1].reshape(LINE, 3 * C), w3[1])
        acc = acc + dot(xs3[r + 2].reshape(LINE, 3 * C), w3[2])
        acc = acc.reshape(FS, COLS, C)
        convf[r] = acc
        st_loc[0, pl.ds(0, FS)] += jnp.sum(acc, axis=1)
        st_loc[0, pl.ds(FS, FS)] += jnp.sum(acc * acc, axis=1)

    st_loc[0] = jnp.zeros((2 * FS, C), F32)
    loads[4].wait()
    loop(1, ROWS - 1, conv_row)

    def edge_start(t):
        line = 1 + t * (ROWS - 2)
        acc = dot(xs3[line].reshape(LINE, 3 * C), w3[1 - t])
        acc = acc + dot(xs3[line + 1].reshape(LINE, 3 * C), w3[2 - t])
        convf[t * (ROWS - 1)] = acc.reshape(FS, COLS, C)

    def edge_finish(t):
        r = t * (ROWS - 1)
        acc = dot(xs3[t * (ROWS + 1)].reshape(LINE, 3 * C), w3[2 * t])
        acc = acc.reshape(FS, COLS, C) + convf[r]
        convf[r] = acc
        st_loc[0, pl.ds(0, FS)] += jnp.sum(acc, axis=1)
        st_loc[0, pl.ds(FS, FS)] += jnp.sum(acc * acc, axis=1)

    loop(0, 2, edge_start)

    def transpose_line(line):
        x = xs3[line, :, :, MID].reshape(LINE, C)
        xt[:, pl.ds(pl.multiple_of(line * LINE, LINE), LINE)] = x.T

    loop(1, ROWS + 1, transpose_line)

    def transpose_w(i):
        for j in range(3):
            wt3[i, pl.ds(j * C, C), :] = w3[i, pl.ds(j * C, C), :].T

    loop(0, 3, transpose_w)
    loads[5].wait()
    for k in range(3):
        tt3[pl.ds(k * C, C), :] = t3[pl.ds(k * C, C), :].T

    not_first = (sp > 0).astype(F32)
    not_last = (sp < NZ - 1).astype(F32)
    halo_x[0].wait_recv()
    widen_row(xs3, 0, 1, not_first)
    halo_x[1].wait_recv()
    widen_row(xs3, ROWS + 1, 1, not_last)
    loop(0, 2, edge_finish)

    def exchange_stats(phase):
        copies = {}
        for o in FAR_FIRST:
            n = phase * (NZ - 1) + o - 1
            copies[o] = remote(
                st_loc.at[phase], st_recv.at[phase, o - 1], ssend.at[n], srecv.at[n],
                (tm, lax.rem(sp + o, NZ)),
            )
        sends.extend(copies.values())
        return copies

    def total_stats(phase, copies):
        total = st_loc[phase]
        for o in range(1, NZ):
            copies[o].wait_recv()
            total = total + st_recv[phase, o - 1]
        return fold8(total) * (1.0 / ENTRIES)

    stats = exchange_stats(0)
    loop(0, 2, lambda t: transpose_line(t * (ROWS + 1)))
    total = total_stats(0, stats)
    mean = total[0:FS]
    variance = total[FS : 2 * FS] - mean * mean
    st_fin[0] = mean
    st_fin[1] = lax.rsqrt(variance + EPS)

    for load in loads[7:]:
        load.wait()
    first = cf[0]
    filled = cf[0] + cf[1]
    gain = gain_ref[...]
    bias = shift_ref[...]

    def activate(f):
        frame = tm * FS + f
        used = (frame < filled).astype(F32)
        v = convf[:, f].reshape(ROWS * COLS, C)
        normed = (v - st_fin[0, pl.ds(f, 1)]) * st_fin[1, pl.ds(f, 1)]
        shaped = normed * gain + bias
        sig = 0.5 * jnp.tanh(0.5 * shaped) + 0.5
        act = shaped * sig * used
        a24[FS + f] = act.astype(BF16).reshape(ROWS, COLS, C)
        convf[:, f] = normed.reshape(ROWS, COLS, C)
        dh[:, f] = (sig * (1.0 + shaped * (1.0 - sig)) * gain).reshape(ROWS, COLS, C)

    def send_activations(part):
        width = FS // 2
        mine = a24.at[pl.ds(FS + part * width, width)]
        later = a24.at[pl.ds(part * width, width)]
        earlier = a24.at[pl.ds(2 * FS + part * width, width)]
        n = 4 + 4 * part
        copies = [
            remote(mine, later, bsend.at[n], brecv.at[n], (tm_next, sp)),
            remote(mine, earlier, bsend.at[n + 1], brecv.at[n + 1], (tm_prev, sp)),
        ]
        sends.extend(copies)
        return copies

    loop(0, FS // 2, activate)
    halo_a = send_activations(0)
    loop(FS // 2, FS, activate)

    def gather(source, f, direction, taps):
        frame = tm * FS + f
        second = (frame >= first).astype(jnp.int32)
        gap = jnp.where(second == 1, dl[1], dl[0])
        for k in taps:
            move = direction * (k - 1) * gap
            target = frame + move
            same = (target >= first).astype(jnp.int32) == second
            live = (frame < filled) & (target >= 0) & (target < filled) & same
            slot = jnp.clip(FS + f + move, 0, 3 * FS - 1)
            keep = jnp.full((ROWS, COLS, C), live.astype(F32)).astype(BF16)
            pieces[f, :, :, pl.ds(k * C, C)] = source[slot] * keep

    loads[6].wait()
    loop(0, FS, lambda f: gather(c24, f, -1, (1,)))
    for copy in halo_c:
        copy.wait_recv()

    def backward_time(f):
        gather(c24, f, -1, (0, 2))
        back = dot(pieces[f].reshape(ROWS * COLS, 3 * C), tt3[...]).astype(BF16).astype(F32)
        grad = back * dh[:, f].reshape(ROWS * COLS, C)
        gn[:, f] = grad.reshape(ROWS, COLS, C)
        normed = convf[:, f].reshape(ROWS * COLS, C)
        st_loc[1, pl.ds(f, 1)] = jnp.sum(grad, axis=0, keepdims=True)
        st_loc[1, pl.ds(FS + f, 1)] = jnp.sum(grad * normed, axis=0, keepdims=True)

    loop(0, FS, backward_time)
    stats = exchange_stats(1)

    first_axis = [(at_y, yi), (at_x, xi), (at_x, xi), (at_y, yi)]
    second_axis = [(at_x, xi), (at_y, yi), (at_y, yi), (at_x, xi)]
    half = C // 2
    stage1 = [None] * 4
    stage2 = [None] * 4
    stage3 = [None] * 4

    theirs = pl.ds(pl.multiple_of((1 - core) * half, half), half)
    mine = pl.ds(pl.multiple_of(core * half, half), half)

    def begin1(b, product):
        s1h[b] = product(theirs).astype(BF16)
        stage1[b] = remote(s1h.at[b], r1.at[b], rsend.at[b, 0], rrecv.at[b, 0], (pair, sp))
        sends.append(stage1[b])

    def begin2(b):
        stage1[b].wait_recv()
        v = wg[b] + r1[b].astype(F32)
        s1[b] = v
        s1c[b] = v.astype(BF16)
        place, index = first_axis[b]
        stage2[b] = []
        for o in range(1, 4):
            rows = pl.ds(pl.multiple_of(lax.rem(index + o, 4) * 32, 32), 32)
            stage2[b].append(
                remote(
                    s1c.at[b, rows, :], r2.at[b, o - 1], rsend.at[b, o], rrecv.at[b, o], (place(o), sp)
                )
            )
        sends.extend(stage2[b])

    def begin3(b):
        index = first_axis[b][1]
        v = s1[b, pl.ds(pl.multiple_of(index * 32, 32), 32), :]
        for o in range(1, 4):
            stage2[b][o - 1].wait_recv()
            v = v + r2[b, o - 1].astype(F32)
        for q in range(4):
            part = v[(q // 2) * 16 : (q // 2) * 16 + 16, (q % 2) * 384 : (q % 2) * 384 + 384]
            s2[b, q] = part
            s2c[b, q] = part.astype(BF16)
        place, index = second_axis[b]
        stage3[b] = []
        for o in range(1, 4):
            stage3[b].append(
                remote(
                    s2c.at[b, lax.rem(index + o, 4)], r3.at[b, o - 1], rsend.at[b, 3 + o],
                    rrecv.at[b, 3 + o], (place(o), sp),
                )
            )
        sends.extend(stage3[b])

    def finish3(b):
        v = s2[b, second_axis[b][1]]
        for o in range(1, 4):
            stage3[b][o - 1].wait_recv()
            v = v + r3[b, o - 1].astype(F32)
        zf[pl.ds(2 * b, 2)] = v.reshape(2, 8, 384)

    def transpose_act(f):
        x = a24[FS + f].reshape(ROWS * COLS, C)
        at[:, pl.ds(pl.multiple_of(f * ROWS * COLS, ROWS * COLS), ROWS * COLS)] = x.T

    loop(0, FS, transpose_act)

    def time_product(rows):
        return dot(at[rows, :], pieces[...].reshape(FS * ROWS * COLS, 3 * C))

    begin1(0, time_product)
    wg[0] = time_product(mine)

    total = total_stats(1, stats)
    st_fin[2] = total[0:FS]
    st_fin[3] = total[FS : 2 * FS]

    def conv_grad(r, f):
        v = st_fin[1, pl.ds(f, 1)] * (
            gn[r, f] - st_fin[2, pl.ds(f, 1)] - convf[r, f] * st_fin[3, pl.ds(f, 1)]
        )
        v16 = v.astype(BF16)
        before, after = shifted(v16.astype(F32))
        gs3[r + 1, f, :, pl.ds(0, C)] = after.astype(BF16)
        gs3[r + 1, f, :, MID] = v16
        gs3[r + 1, f, :, pl.ds(2 * C, C)] = before.astype(BF16)

    def conv_grad_edges(f):
        conv_grad(0, f)
        conv_grad(ROWS - 1, f)

    def conv_grad_inner(f):
        conv_grad(1, f)
        conv_grad(2, f)

    loop(0, FS, conv_grad_edges)
    halo_g = [
        remote(gs3.at[ROWS, :, :, MID], gs3.at[0, :, :, MID], bsend.at[6], brecv.at[6], (tm, sp_next)),
        remote(gs3.at[1, :, :, MID], gs3.at[ROWS + 1, :, :, MID], bsend.at[7], brecv.at[7], (tm, sp_prev)),
    ]
    sends += halo_g
    loop(0, FS, conv_grad_inner)
    begin2(0)

    def space_product(i, rows):
        return dot(
            xt[rows, pl.ds(i * LINE, ROWS * LINE)], gs3[pl.ds(1, ROWS)].reshape(ROWS * LINE, 3 * C)
        )

    for i in range(3):
        begin1(i + 1, functools.partial(space_product, i))
    for i in range(3):
        wg[i + 1] = space_product(i, mine)
        begin2(i + 1)
    begin3(0)

    def in_row(r):
        acc = dot(gs3[r + 2].reshape(LINE, 3 * C), wt3[0])
        acc = acc + dot(gs3[r + 1].reshape(LINE, 3 * C), wt3[1])
        acc = acc + dot(gs3[r].reshape(LINE, 3 * C), wt3[2])
        acc = acc.reshape(FS, COLS, C) + c24[pl.ds(FS, FS), r].astype(F32)
        outv[0, :, r] = acc.astype(BF16)

    loop(1, ROWS - 1, in_row)
    for b in (1, 2, 3):
        begin3(b)
    halo_g[0].wait_recv()
    widen_row(gs3, 0, -1, not_first)
    halo_g[1].wait_recv()
    widen_row(gs3, ROWS + 1, -1, not_last)
    for b in range(4):
        finish3(b)
    z1 = {}
    for o in FAR_FIRST:
        q = lax.rem(sp + o, NZ)
        z1[o] = (remote(zf.at[q], zrecv.at[o - 1], ssend.at[13 + o], srecv.at[13 + o], (tm, q)))
    sends += z1.values()
    halo_a += send_activations(1)
    loop(0, 2, lambda t: in_row(t * (ROWS - 1)))
    out_ig = pltpu.make_async_copy(outv.at[0], ig_out, lsem.at[7])
    out_ig.start()

    v = zf[sp]
    for o in range(1, NZ):
        z1[o].wait_recv()
        v = v + zrecv[o - 1]
    zag[sp] = v
    z2 = []
    for o in FAR_FIRST:
        q = lax.rem(sp + o, NZ)
        z2.append(remote(zag.at[sp], zag.at[sp], ssend.at[20 + o], srecv.at[20 + o], (tm, q)))
    sends += z2

    def forward_time(f):
        gather(a24, f, 1, (0, 1, 2))
        moved = dot(pieces[f].reshape(ROWS * COLS, 3 * C), t3[...]).astype(BF16).astype(F32)
        x = xs3[pl.ds(1, ROWS), f, :, MID].astype(F32)
        outv[1, f] = (x + moved.reshape(ROWS, COLS, C)).astype(BF16)

    early_sends = sends
    sends = []
    for copy in z2:
        copy.wait_recv()
    g3 = []
    for b in range(4):
        n1, n2 = first_axis[b][1], second_axis[b][1]
        agb[b, core, n1, n2] = zag[pl.ds(2 * b, 2)].reshape(16, 384).astype(BF16)
        place = second_axis[b][0]
        here = agb.at[b, core, n1, n2]
        g3.append(
            [remote(here, here, rsend.at[b, 6 + o], rrecv.at[b, 6 + o], (place(o), sp)) for o in (2, 1, 3)]
        )
        sends += g3[b]
    g2 = [{} for _ in range(4)]
    for c in (0, 1, 3, 2):
        for b in range(4):
            if c > 0:
                g3[b][(2, 1, 3).index(c)].wait_recv()
            place, n1 = first_axis[b]
            here = agb.at[b, core, n1, lax.rem(second_axis[b][1] + 4 - c, 4)]
            for o in (2, 1, 3):
                n = 6 + 4 * o + c
                g2[b][o, c] = remote(here, here, rsend.at[b, n], rrecv.at[b, n], (place(o), sp))
            sends += [g2[b][o, c] for o in (2, 1, 3)]
        if c == 0:
            for copy in early_sends:
                copy.wait_send()
            for copy in halo_a:
                copy.wait_recv()
            loop(0, FS, forward_time)
            out_t = pltpu.make_async_copy(outv.at[1], tout, lsem.at[8])
            out_t.start()
    g1 = []
    out_g = []
    for o in (0, 1, 3, 2):
        for b in range(4):
            if o > 0:
                for c in (0, 1, 3, 2):
                    g2[b][o, c].wait_recv()
            here = lax.rem(first_axis[b][1] + 4 - o, 4)
            g1.append(
                remote(
                    agb.at[b, core, here], ag_out.at[b, core, here], rsend.at[b, 22 + o],
                    rrecv.at[b, 22 + o], (pair, sp),
                )
            )
            out_g.append(
                pltpu.make_async_copy(agb.at[b, core, here], ag_out.at[b, core, here], osem.at[b, o])
            )
            out_g[-1].start()
    for copy in sends:
        copy.wait_send()
    for copy in g1:
        copy.wait()
    out_ig.wait()
    out_t.wait()
    for copy in out_g:
        copy.wait()


def deliver(of_in, ig_in, ag, of, ig, sg, tg, agv, full, frames, csem, gsem):
    loads = [pltpu.make_async_copy(ag.at[b], agv.at[b], gsem.at[b]) for b in range(4)]
    for load in loads:
        load.start()
    quarter = FS // 4
    parts = []
    for n in range(4):
        part = pl.ds(n * quarter, quarter)
        parts.append((of_in.at[part], frames.at[0, part], of.at[part], csem.at[0, n]))
        parts.append((ig_in.at[part], frames.at[1, part], ig.at[part], csem.at[1, n]))
    arrivals = [pltpu.make_async_copy(source, stage, sem) for source, stage, _, sem in parts]
    for copy in arrivals:
        copy.start()
    stores = []
    for b in range(4):
        loads[b].wait()

        def place(m, carry):
            for q in range(4):
                rows = pl.ds(pl.multiple_of(m * 32 + (q // 2) * 16, 16), 16)
                v = agv[b, lax.div(m, 4), lax.rem(m, 4), q].astype(F32)
                if q % 2 == 0:
                    full[3 * b, rows, :] = v[:, 0:C]
                    full[3 * b + 1, rows, pl.ds(0, 128)] = v[:, C:384]
                else:
                    full[3 * b + 1, rows, pl.ds(128, 128)] = v[:, 0:128]
                    full[3 * b + 2, rows, :] = v[:, 128:384]
            return carry

        lax.fori_loop(0, 8, place, 0)
        target = tg if b == 0 else sg.at[pl.ds(3 * (b - 1), 3)]
        stores.append(pltpu.make_async_copy(full.at[pl.ds(3 * b, 3)], target, gsem.at[b]))
        stores[b].start()
    copies = []
    for copy, (_, stage, target, sem) in zip(arrivals, parts):
        copy.wait()
        copies.append(pltpu.make_async_copy(stage, target, sem))
        copies[-1].start()
    for copy in copies + stores:
        copy.wait()


def section(frames_in, cotangent, spatial, temporal, norm_gain, norm_shift, clip_frames, dilation):
    any_spec = pl.BlockSpec(memory_space=pl.ANY)
    shape = (FS, ROWS, COLS, C)
    V = pltpu.VMEM
    DMA = pltpu.SemaphoreType.DMA
    tout, ig, ag = pl.pallas_call(
        kernel,
        out_shape=(
            jax.ShapeDtypeStruct(shape, BF16),
            jax.ShapeDtypeStruct(shape, BF16),
            jax.ShapeDtypeStruct((4, 2, 4, 4, 16, 384), BF16),
        ),
        in_specs=[any_spec] * 8,
        out_specs=(any_spec, any_spec, any_spec),
        scratch_shapes=[
            V((ROWS + 2, FS, COLS, 3 * C), BF16),
            V((C, (ROWS + 2) * LINE), BF16),
            V((ROWS, FS, COLS, C), F32),
            V((ROWS, FS, COLS, C), F32),
            V((ROWS, FS, COLS, C), F32),
            V((3 * FS, ROWS, COLS, C), BF16),
            V((3 * FS, ROWS, COLS, C), BF16),
            V((FS, ROWS, COLS, 3 * C), BF16),
            V((C, FS * ROWS * COLS), BF16),
            V((ROWS + 2, FS, COLS, 3 * C), BF16),
            V((3, 3 * C, C), BF16),
            V((3, 3 * C, C), BF16),
            V((3 * C, C), BF16),
            V((3 * C, C), BF16),
            V((2, 2 * FS, C), F32),
            V((2, NZ - 1, 2 * FS, C), F32),
            V((4, FS, C), F32),
            V((4, C // 2, 3 * C), F32),
            V((4, C // 2, 3 * C), BF16),
            V((4, C // 2, 3 * C), BF16),
            V((4, C // 2, 3 * C), F32),
            V((4, C // 2, 3 * C), BF16),
            V((4, 3, 32, 3 * C), BF16),
            V((4, 4, 16, 384), F32),
            V((4, 4, 16, 384), BF16),
            V((4, 3, 16, 384), BF16),
            V((NZ, 8, 384), F32),
            V((NZ - 1, 8, 384), F32),
            V((NZ, 8, 384), F32),
            V((4, 2, 4, 4, 16, 384), BF16),
            V((2,) + shape, BF16),
            V((1, C), F32),
            V((1, C), F32),
            pltpu.SMEM((2,), jnp.int32),
            pltpu.SMEM((2,), jnp.int32),
            DMA((13,)),
            DMA((4, 4)),
            DMA((10,)),
            DMA((10,)),
            DMA((28,)),
            DMA((28,)),
            DMA((4, 26)),
            DMA((4, 26)),
        ],
        compiler_params=pltpu.CompilerParams(
            collective_id=0, has_side_effects=True, vmem_limit_bytes=58 * 1024 * 1024
        ),
        cost_estimate=pl.CostEstimate(flops=9_700_000_000, bytes_accessed=9_000_000, transcendentals=0),
    )(
        frames_in,
        cotangent,
        spatial.reshape(3, 3 * C, C),
        temporal.reshape(3 * C, C),
        norm_gain.reshape(1, C),
        norm_shift.reshape(1, C),
        clip_frames,
        dilation,
    )
    out_frames, in_grad, spatial_grad, temporal_grad = pl.pallas_call(
        deliver,
        out_shape=(
            jax.ShapeDtypeStruct(shape, BF16),
            jax.ShapeDtypeStruct(shape, BF16),
            jax.ShapeDtypeStruct((9, C, C), F32),
            jax.ShapeDtypeStruct((3, C, C), F32),
        ),
        in_specs=[any_spec] * 3,
        out_specs=(any_spec,) * 4,
        scratch_shapes=[V((4, 2, 4, 4, 16, 384), BF16), V((12, C, C), F32), V((2,) + shape, BF16), DMA((2, 4)), DMA((4,))],
        compiler_params=pltpu.CompilerParams(vmem_limit_bytes=58 * 1024 * 1024),
        cost_estimate=pl.CostEstimate(flops=0, bytes_accessed=9_000_000, transcendentals=0),
    )(tout, ig, ag)
    return out_frames, in_grad, spatial_grad.reshape(3, 3, C, C), temporal_grad


def solution(mesh):
    frames = P("tm", "space", None, None)
    return jax.shard_map(
        section,
        mesh=mesh,
        in_specs=(frames, frames, P(), P(), P(), P(), P(), P()),
        out_specs=(frames, frames, P(), P()),
        check_vma=False,
    )
```

```python
import functools

import jax
import jax.numpy as jnp
from jax import lax
from jax.experimental import pallas as pl
from jax.experimental.pallas import tpu as pltpu
from jax.sharding import PartitionSpec as P

MESH = pl.DeviceIdType.MESH
F32 = jnp.float32
BF16 = jnp.bfloat16
C = 256
FS = 8
ROWS = 4
COLS = 64
NX = 4
NY = 4
NTM = 32
NZ = 8
LINE = FS * COLS
ENTRIES = float(ROWS * NZ * COLS * 8)
EPS = 1e-05
MID = pl.ds(C, C)
FAR_FIRST = (4, 3, 5, 2, 6, 1, 7)


def dot(a, b):
    return jnp.dot(a, b, preferred_element_type=F32)


def fold8(v):
    lane = lax.broadcasted_iota(jnp.int32, v.shape, 1)
    for step in (1, 2, 4):
        low = pltpu.roll(v, C - step, 1)
        high = pltpu.roll(v, step, 1)
        v = v + jnp.where((lane & step) == 0, low, high)
    return v


def shifted(v):
    n = v.shape[0]
    col = lax.broadcasted_iota(jnp.int32, v.shape, 0) & (COLS - 1)
    before = jnp.where(col == 0, 0.0, pltpu.roll(v, 1, 0))
    after = jnp.where(col == COLS - 1, 0.0, pltpu.roll(v, n - 1, 0))
    return before, after


def kernel(
    fr, ct, w_in, t_in, gain_in, shift_in, cf_in, dl_in,
    tout, ig_out, ag_out,
    xs3, xt, convf, dh, gn, a24, c24, pieces, at, gs3, w3, wt3, t3, tt3,
    st_loc, st_recv, st_fin, wg, s1h, r1, s1, s1c, r2, s2, s2c, r3, zf, zrecv, zag, agb, outv,
    gain_ref, shift_ref, cf, dl,
    lsem, osem, bsend, brecv, ssend, srecv, rsend, rrecv,
):
    tm = lax.axis_index("tm")
    sp = lax.axis_index("space")
    core = lax.rem(tm, 2)
    yi = lax.rem(lax.div(tm, 2), NY)
    xi = lax.div(tm, 2 * NY)
    pair = tm + 1 - 2 * core
    tm_next = lax.rem(tm + 1, NTM)
    tm_prev = lax.rem(tm + NTM - 1, NTM)
    sp_next = lax.rem(sp + 1, NZ)
    sp_prev = lax.rem(sp + NZ - 1, NZ)

    def at_x(o):
        return (lax.rem(xi + o, NX) * NY + yi) * 2 + core

    def at_y(o):
        return (xi * NY + lax.rem(yi + o, NY)) * 2 + core

    def remote(src, dst, send, recv, device):
        copy = pltpu.make_async_remote_copy(
            src_ref=src, dst_ref=dst, send_sem=send, recv_sem=recv, device_id=device, device_id_type=MESH
        )
        copy.start()
        return copy

    far = tm + (2 * core - 1)
    far = lax.rem(far + NTM, NTM)
    partners = [(pair, sp), (far, sp)]
    partners += [(tm, lax.rem(sp + o, NZ)) for o in range(1, NZ)]
    partners += [(at_x(o), sp) for o in range(1, NX)]
    partners += [(at_y(o), sp) for o in range(1, NY)]
    barrier = pltpu.get_barrier_semaphore()
    for partner in partners:
        pl.semaphore_signal(barrier, inc=1, device_id=partner, device_id_type=MESH)
    loads = [
        pltpu.make_async_copy(fr.at[:, r], xs3.at[r + 1, :, :, MID], lsem.at[r]) for r in range(ROWS)
    ]
    loads.append(pltpu.make_async_copy(w_in, w3, lsem.at[4]))
    loads.append(pltpu.make_async_copy(t_in, t3, lsem.at[5]))
    loads.append(pltpu.make_async_copy(ct, c24.at[pl.ds(FS, FS)], lsem.at[6]))
    small = [(gain_in, gain_ref), (shift_in, shift_ref), (cf_in, cf), (dl_in, dl)]
    loads += [pltpu.make_async_copy(source, target, lsem.at[9 + n]) for n, (source, target) in enumerate(small)]
    for load in loads:
        load.start()

    pl.semaphore_wait(barrier, len(partners))

    sends = []
    halo_x = [
        remote(fr.at[:, ROWS - 1], xs3.at[0, :, :, MID], bsend.at[0], brecv.at[0], (tm, sp_next)),
        remote(fr.at[:, 0], xs3.at[ROWS + 1, :, :, MID], bsend.at[1], brecv.at[1], (tm, sp_prev)),
    ]
    halo_c = [
        remote(ct, c24.at[pl.ds(0, FS)], bsend.at[2], brecv.at[2], (tm_next, sp)),
        remote(ct, c24.at[pl.ds(2 * FS, FS)], bsend.at[3], brecv.at[3], (tm_prev, sp)),
    ]
    sends += halo_x + halo_c

    def widen_row(ref, line, order, keep):
        v = ref[line, :, :, MID].reshape(LINE, C).astype(F32)
        if keep is not None:
            v = v * keep
            ref[line, :, :, MID] = v.astype(BF16).reshape(FS, COLS, C)
        before, after = shifted(v)
        if order < 0:
            before, after = after, before
        ref[line, :, :, pl.ds(0, C)] = before.astype(BF16).reshape(FS, COLS, C)
        ref[line, :, :, pl.ds(2 * C, C)] = after.astype(BF16).reshape(FS, COLS, C)

    def loop(lo, hi, body):
        def step(i, carry):
            body(i)
            return carry

        lax.fori_loop(lo, hi, step, 0)

    for r in range(ROWS):
        loads[r].wait()
    loop(1, ROWS + 1, lambda line: widen_row(xs3, line, 1, None))

    def conv_row(r):
        acc = dot(xs3[r].reshape(LINE, 3 * C), w3[0])
        acc = acc + dot(xs3[r + 1].reshape(LINE, 3 * C), w3[1])
        acc = acc + dot(xs3[r + 2].reshape(LINE, 3 * C), w3[2])
        acc = acc.reshape(FS, COLS, C)
        convf[r] = acc
        st_loc[0, pl.ds(0, FS)] += jnp.sum(acc, axis=1)
        st_loc[0, pl.ds(FS, FS)] += jnp.sum(acc * acc, axis=1)

    st_loc[0] = jnp.zeros((2 * FS, C), F32)
    loads[4].wait()
    loop(1, ROWS - 1, conv_row)

    def edge_start(t):
        line = 1 + t * (ROWS - 2)
        acc = dot(xs3[line].reshape(LINE, 3 * C), w3[1 - t])
        acc = acc + dot(xs3[line + 1].reshape(LINE, 3 * C), w3[2 - t])
        convf[t * (ROWS - 1)] = acc.reshape(FS, COLS, C)

    def edge_finish(t):
        r = t * (ROWS - 1)
        acc = dot(xs3[t * (ROWS + 1)].reshape(LINE, 3 * C), w3[2 * t])
        acc = acc.reshape(FS, COLS, C) + convf[r]
        convf[r] = acc
        st_loc[0, pl.ds(0, FS)] += jnp.sum(acc, axis=1)
        st_loc[0, pl.ds(FS, FS)] += jnp.sum(acc * acc, axis=1)

    loop(0, 2, edge_start)

    def transpose_line(line):
        x = xs3[line, :, :, MID].reshape(LINE, C)
        xt[:, pl.ds(pl.multiple_of(line * LINE, LINE), LINE)] = x.T

    loop(1, ROWS + 1, transpose_line)

    def transpose_w(i):
        for j in range(3):
            wt3[i, pl.ds(j * C, C), :] = w3[i, pl.ds(j * C, C), :].T

    loop(0, 3, transpose_w)
    loads[5].wait()
    for k in range(3):
        tt3[pl.ds(k * C, C), :] = t3[pl.ds(k * C, C), :].T

    not_first = (sp > 0).astype(F32)
    not_last = (sp < NZ - 1).astype(F32)
    halo_x[0].wait_recv()
    widen_row(xs3, 0, 1, not_first)
    halo_x[1].wait_recv()
    widen_row(xs3, ROWS + 1, 1, not_last)
    loop(0, 2, edge_finish)

    def exchange_stats(phase):
        copies = {}
        for o in FAR_FIRST:
            n = phase * (NZ - 1) + o - 1
            copies[o] = remote(
                st_loc.at[phase], st_recv.at[phase, o - 1], ssend.at[n], srecv.at[n],
                (tm, lax.rem(sp + o, NZ)),
            )
        sends.extend(copies.values())
        return copies

    def total_stats(phase, copies):
        total = st_loc[phase]
        for o in range(1, NZ):
            copies[o].wait_recv()
            total = total + st_recv[phase, o - 1]
        return fold8(total) * (1.0 / ENTRIES)

    stats = exchange_stats(0)
    loop(0, 2, lambda t: transpose_line(t * (ROWS + 1)))
    total = total_stats(0, stats)
    mean = total[0:FS]
    variance = total[FS : 2 * FS] - mean * mean
    st_fin[0] = mean
    st_fin[1] = lax.rsqrt(variance + EPS)

    for load in loads[7:]:
        load.wait()
    first = cf[0]
    filled = cf[0] + cf[1]
    gain = gain_ref[...]
    bias = shift_ref[...]

    def activate(f):
        frame = tm * FS + f
        used = (frame < filled).astype(F32)
        v = convf[:, f].reshape(ROWS * COLS, C)
        normed = (v - st_fin[0, pl.ds(f, 1)]) * st_fin[1, pl.ds(f, 1)]
        shaped = normed * gain + bias
        sig = 0.5 * jnp.tanh(0.5 * shaped) + 0.5
        act = shaped * sig * used
        a24[FS + f] = act.astype(BF16).reshape(ROWS, COLS, C)
        convf[:, f] = normed.reshape(ROWS, COLS, C)
        dh[:, f] = (sig * (1.0 + shaped * (1.0 - sig)) * gain).reshape(ROWS, COLS, C)

    def send_activations(part):
        width = FS // 2
        mine = a24.at[pl.ds(FS + part * width, width)]
        later = a24.at[pl.ds(part * width, width)]
        earlier = a24.at[pl.ds(2 * FS + part * width, width)]
        n = 4 + 4 * part
        copies = [
            remote(mine, later, bsend.at[n], brecv.at[n], (tm_next, sp)),
            remote(mine, earlier, bsend.at[n + 1], brecv.at[n + 1], (tm_prev, sp)),
        ]
        sends.extend(copies)
        return copies

    loop(0, FS // 2, activate)
    halo_a = send_activations(0)
    loop(FS // 2, FS, activate)

    def gather(source, f, direction, taps):
        frame = tm * FS + f
        second = (frame >= first).astype(jnp.int32)
        gap = jnp.where(second == 1, dl[1], dl[0])
        for k in taps:
            move = direction * (k - 1) * gap
            target = frame + move
            same = (target >= first).astype(jnp.int32) == second
            live = (frame < filled) & (target >= 0) & (target < filled) & same
            slot = jnp.clip(FS + f + move, 0, 3 * FS - 1)
            keep = jnp.full((ROWS, COLS, C), live.astype(F32)).astype(BF16)
            pieces[f, :, :, pl.ds(k * C, C)] = source[slot] * keep

    loads[6].wait()
    loop(0, FS, lambda f: gather(c24, f, -1, (1,)))
    for copy in halo_c:
        copy.wait_recv()

    def backward_time(f):
        gather(c24, f, -1, (0, 2))
        back = dot(pieces[f].reshape(ROWS * COLS, 3 * C), tt3[...]).astype(BF16).astype(F32)
        grad = back * dh[:, f].reshape(ROWS * COLS, C)
        gn[:, f] = grad.reshape(ROWS, COLS, C)
        normed = convf[:, f].reshape(ROWS * COLS, C)
        st_loc[1, pl.ds(f, 1)] = jnp.sum(grad, axis=0, keepdims=True)
        st_loc[1, pl.ds(FS + f, 1)] = jnp.sum(grad * normed, axis=0, keepdims=True)

    loop(0, FS, backward_time)
    stats = exchange_stats(1)

    first_axis = [(at_y, yi), (at_x, xi), (at_x, xi), (at_y, yi)]
    second_axis = [(at_x, xi), (at_y, yi), (at_y, yi), (at_x, xi)]
    half = C // 2
    stage1 = [None] * 4
    stage2 = [None] * 4
    stage3 = [None] * 4

    theirs = pl.ds(pl.multiple_of((1 - core) * half, half), half)
    mine = pl.ds(pl.multiple_of(core * half, half), half)

    def begin1(b, product):
        s1h[b] = product(theirs).astype(BF16)
        stage1[b] = remote(s1h.at[b], r1.at[b], rsend.at[b, 0], rrecv.at[b, 0], (pair, sp))
        sends.append(stage1[b])

    def begin2(b):
        stage1[b].wait_recv()
        v = wg[b] + r1[b].astype(F32)
        s1[b] = v
        s1c[b] = v.astype(BF16)
        place, index = first_axis[b]
        stage2[b] = []
        for o in range(1, 4):
            rows = pl.ds(pl.multiple_of(lax.rem(index + o, 4) * 32, 32), 32)
            stage2[b].append(
                remote(
                    s1c.at[b, rows, :], r2.at[b, o - 1], rsend.at[b, o], rrecv.at[b, o], (place(o), sp)
                )
            )
        sends.extend(stage2[b])

    def begin3(b):
        index = first_axis[b][1]
        v = s1[b, pl.ds(pl.multiple_of(index * 32, 32), 32), :]
        for o in range(1, 4):
            stage2[b][o - 1].wait_recv()
            v = v + r2[b, o - 1].astype(F32)
        for q in range(4):
            part = v[(q // 2) * 16 : (q // 2) * 16 + 16, (q % 2) * 384 : (q % 2) * 384 + 384]
            s2[b, q] = part
            s2c[b, q] = part.astype(BF16)
        place, index = second_axis[b]
        stage3[b] = []
        for o in range(1, 4):
            stage3[b].append(
                remote(
                    s2c.at[b, lax.rem(index + o, 4)], r3.at[b, o - 1], rsend.at[b, 3 + o],
                    rrecv.at[b, 3 + o], (place(o), sp),
                )
            )
        sends.extend(stage3[b])

    def finish3(b):
        v = s2[b, second_axis[b][1]]
        for o in range(1, 4):
            stage3[b][o - 1].wait_recv()
            v = v + r3[b, o - 1].astype(F32)
        zf[pl.ds(2 * b, 2)] = v.reshape(2, 8, 384)

    def transpose_act(f):
        x = a24[FS + f].reshape(ROWS * COLS, C)
        at[:, pl.ds(pl.multiple_of(f * ROWS * COLS, ROWS * COLS), ROWS * COLS)] = x.T

    loop(0, FS, transpose_act)

    def time_product(rows):
        return dot(at[rows, :], pieces[...].reshape(FS * ROWS * COLS, 3 * C))

    begin1(0, time_product)
    wg[0] = time_product(mine)

    total = total_stats(1, stats)
    st_fin[2] = total[0:FS]
    st_fin[3] = total[FS : 2 * FS]

    def conv_grad(r, f):
        v = st_fin[1, pl.ds(f, 1)] * (
            gn[r, f] - st_fin[2, pl.ds(f, 1)] - convf[r, f] * st_fin[3, pl.ds(f, 1)]
        )
        v16 = v.astype(BF16)
        before, after = shifted(v16.astype(F32))
        gs3[r + 1, f, :, pl.ds(0, C)] = after.astype(BF16)
        gs3[r + 1, f, :, MID] = v16
        gs3[r + 1, f, :, pl.ds(2 * C, C)] = before.astype(BF16)

    def conv_grad_edges(f):
        conv_grad(0, f)
        conv_grad(ROWS - 1, f)

    def conv_grad_inner(f):
        conv_grad(1, f)
        conv_grad(2, f)

    loop(0, FS, conv_grad_edges)
    halo_g = [
        remote(gs3.at[ROWS, :, :, MID], gs3.at[0, :, :, MID], bsend.at[6], brecv.at[6], (tm, sp_next)),
        remote(gs3.at[1, :, :, MID], gs3.at[ROWS + 1, :, :, MID], bsend.at[7], brecv.at[7], (tm, sp_prev)),
    ]
    sends += halo_g
    loop(0, FS, conv_grad_inner)
    begin2(0)

    def space_product(i, rows):
        return dot(
            xt[rows, pl.ds(i * LINE, ROWS * LINE)], gs3[pl.ds(1, ROWS)].reshape(ROWS * LINE, 3 * C)
        )

    for i in range(3):
        begin1(i + 1, functools.partial(space_product, i))
    for i in range(3):
        wg[i + 1] = space_product(i, mine)
        begin2(i + 1)
    begin3(0)

    def in_row(r):
        acc = dot(gs3[r + 2].reshape(LINE, 3 * C), wt3[0])
        acc = acc + dot(gs3[r + 1].reshape(LINE, 3 * C), wt3[1])
        acc = acc + dot(gs3[r].reshape(LINE, 3 * C), wt3[2])
        acc = acc.reshape(FS, COLS, C) + c24[pl.ds(FS, FS), r].astype(F32)
        outv[0, :, r] = acc.astype(BF16)

    loop(1, ROWS - 1, in_row)
    for b in (1, 2, 3):
        begin3(b)
    halo_g[0].wait_recv()
    widen_row(gs3, 0, -1, not_first)
    halo_g[1].wait_recv()
    widen_row(gs3, ROWS + 1, -1, not_last)
    for b in range(4):
        finish3(b)
    z1 = {}
    for o in FAR_FIRST:
        q = lax.rem(sp + o, NZ)
        z1[o] = (remote(zf.at[q], zrecv.at[o - 1], ssend.at[13 + o], srecv.at[13 + o], (tm, q)))
    sends += z1.values()
    halo_a += send_activations(1)
    loop(0, 2, lambda t: in_row(t * (ROWS - 1)))
    out_ig = pltpu.make_async_copy(outv.at[0], ig_out, lsem.at[7])
    out_ig.start()

    v = zf[sp]
    for o in range(1, NZ):
        z1[o].wait_recv()
        v = v + zrecv[o - 1]
    zag[sp] = v
    z2 = []
    for o in FAR_FIRST:
        q = lax.rem(sp + o, NZ)
        z2.append(remote(zag.at[sp], zag.at[sp], ssend.at[20 + o], srecv.at[20 + o], (tm, q)))
    sends += z2

    def forward_time(f):
        gather(a24, f, 1, (0, 1, 2))
        moved = dot(pieces[f].reshape(ROWS * COLS, 3 * C), t3[...]).astype(BF16).astype(F32)
        x = xs3[pl.ds(1, ROWS), f, :, MID].astype(F32)
        outv[1, f] = (x + moved.reshape(ROWS, COLS, C)).astype(BF16)

    early_sends = sends
    sends = []
    for copy in z2:
        copy.wait_recv()
    g3 = []
    for b in range(4):
        n1, n2 = first_axis[b][1], second_axis[b][1]
        agb[b, core, n1, n2] = zag[pl.ds(2 * b, 2)].reshape(16, 384).astype(BF16)
        place = second_axis[b][0]
        here = agb.at[b, core, n1, n2]
        g3.append(
            [remote(here, here, rsend.at[b, 6 + o], rrecv.at[b, 6 + o], (place(o), sp)) for o in (2, 1, 3)]
        )
        sends += g3[b]
    g2 = [{} for _ in range(4)]
    for c in (0, 1, 3, 2):
        for b in range(4):
            if c > 0:
                g3[b][(2, 1, 3).index(c)].wait_recv()
            place, n1 = first_axis[b]
            here = agb.at[b, core, n1, lax.rem(second_axis[b][1] + 4 - c, 4)]
            for o in (2, 1, 3):
                n = 6 + 4 * o + c
                g2[b][o, c] = remote(here, here, rsend.at[b, n], rrecv.at[b, n], (place(o), sp))
            sends += [g2[b][o, c] for o in (2, 1, 3)]
        if c == 0:
            for copy in halo_a:
                copy.wait_recv()
            loop(0, FS, forward_time)
            out_t = pltpu.make_async_copy(outv.at[1], tout, lsem.at[8])
            out_t.start()
    g1 = []
    out_g = []
    for o in (0, 1, 3, 2):
        for b in range(4):
            if o > 0:
                for c in (0, 1, 3, 2):
                    g2[b][o, c].wait_recv()
            here = lax.rem(first_axis[b][1] + 4 - o, 4)
            g1.append(
                remote(
                    agb.at[b, core, here], ag_out.at[b, core, here], rsend.at[b, 22 + o],
                    rrecv.at[b, 22 + o], (pair, sp),
                )
            )
            out_g.append(
                pltpu.make_async_copy(agb.at[b, core, here], ag_out.at[b, core, here], osem.at[b, o])
            )
            out_g[-1].start()
    for copy in early_sends + sends:
        copy.wait_send()
    for copy in g1:
        copy.wait()
    out_ig.wait()
    out_t.wait()
    for copy in out_g:
        copy.wait()


def deliver(of_in, ig_in, ag, of, ig, sg, tg, agv, full, frames, csem, gsem):
    loads = [pltpu.make_async_copy(ag.at[b], agv.at[b], gsem.at[b]) for b in range(4)]
    for load in loads:
        load.start()
    quarter = FS // 4
    parts = []
    for n in range(4):
        part = pl.ds(n * quarter, quarter)
        parts.append((of_in.at[part], frames.at[0, part], of.at[part], csem.at[0, n]))
        parts.append((ig_in.at[part], frames.at[1, part], ig.at[part], csem.at[1, n]))
    arrivals = [pltpu.make_async_copy(source, stage, sem) for source, stage, _, sem in parts]
    for copy in arrivals:
        copy.start()
    stores = []
    for b in range(4):
        loads[b].wait()

        def place(m, carry):
            for q in range(4):
                rows = pl.ds(pl.multiple_of(m * 32 + (q // 2) * 16, 16), 16)
                v = agv[b, lax.div(m, 4), lax.rem(m, 4), q].astype(F32)
                if q % 2 == 0:
                    full[3 * b, rows, :] = v[:, 0:C]
                    full[3 * b + 1, rows, pl.ds(0, 128)] = v[:, C:384]
                else:
                    full[3 * b + 1, rows, pl.ds(128, 128)] = v[:, 0:128]
                    full[3 * b + 2, rows, :] = v[:, 128:384]
            return carry

        lax.fori_loop(0, 8, place, 0)
        target = tg if b == 0 else sg.at[pl.ds(3 * (b - 1), 3)]
        stores.append(pltpu.make_async_copy(full.at[pl.ds(3 * b, 3)], target, gsem.at[b]))
        stores[b].start()
    copies = []
    for copy, (_, stage, target, sem) in zip(arrivals, parts):
        copy.wait()
        copies.append(pltpu.make_async_copy(stage, target, sem))
        copies[-1].start()
    for copy in copies + stores:
        copy.wait()


def section(frames_in, cotangent, spatial, temporal, norm_gain, norm_shift, clip_frames, dilation):
    any_spec = pl.BlockSpec(memory_space=pl.ANY)
    shape = (FS, ROWS, COLS, C)
    V = pltpu.VMEM
    DMA = pltpu.SemaphoreType.DMA
    tout, ig, ag = pl.pallas_call(
        kernel,
        out_shape=(
            jax.ShapeDtypeStruct(shape, BF16),
            jax.ShapeDtypeStruct(shape, BF16),
            jax.ShapeDtypeStruct((4, 2, 4, 4, 16, 384), BF16),
        ),
        in_specs=[any_spec] * 8,
        out_specs=(any_spec, any_spec, any_spec),
        scratch_shapes=[
            V((ROWS + 2, FS, COLS, 3 * C), BF16),
            V((C, (ROWS + 2) * LINE), BF16),
            V((ROWS, FS, COLS, C), F32),
            V((ROWS, FS, COLS, C), F32),
            V((ROWS, FS, COLS, C), F32),
            V((3 * FS, ROWS, COLS, C), BF16),
            V((3 * FS, ROWS, COLS, C), BF16),
            V((FS, ROWS, COLS, 3 * C), BF16),
            V((C, FS * ROWS * COLS), BF16),
            V((ROWS + 2, FS, COLS, 3 * C), BF16),
            V((3, 3 * C, C), BF16),
            V((3, 3 * C, C), BF16),
            V((3 * C, C), BF16),
            V((3 * C, C), BF16),
            V((2, 2 * FS, C), F32),
            V((2, NZ - 1, 2 * FS, C), F32),
            V((4, FS, C), F32),
            V((4, C // 2, 3 * C), F32),
            V((4, C // 2, 3 * C), BF16),
            V((4, C // 2, 3 * C), BF16),
            V((4, C // 2, 3 * C), F32),
            V((4, C // 2, 3 * C), BF16),
            V((4, 3, 32, 3 * C), BF16),
            V((4, 4, 16, 384), F32),
            V((4, 4, 16, 384), BF16),
            V((4, 3, 16, 384), BF16),
            V((NZ, 8, 384), F32),
            V((NZ - 1, 8, 384), F32),
            V((NZ, 8, 384), F32),
            V((4, 2, 4, 4, 16, 384), BF16),
            V((2,) + shape, BF16),
            V((1, C), F32),
            V((1, C), F32),
            pltpu.SMEM((2,), jnp.int32),
            pltpu.SMEM((2,), jnp.int32),
            DMA((13,)),
            DMA((4, 4)),
            DMA((10,)),
            DMA((10,)),
            DMA((28,)),
            DMA((28,)),
            DMA((4, 26)),
            DMA((4, 26)),
        ],
        compiler_params=pltpu.CompilerParams(
            collective_id=0, has_side_effects=True, vmem_limit_bytes=58 * 1024 * 1024
        ),
        cost_estimate=pl.CostEstimate(flops=9_700_000_000, bytes_accessed=9_000_000, transcendentals=0),
    )(
        frames_in,
        cotangent,
        spatial.reshape(3, 3 * C, C),
        temporal.reshape(3 * C, C),
        norm_gain.reshape(1, C),
        norm_shift.reshape(1, C),
        clip_frames,
        dilation,
    )
    out_frames, in_grad, spatial_grad, temporal_grad = pl.pallas_call(
        deliver,
        out_shape=(
            jax.ShapeDtypeStruct(shape, BF16),
            jax.ShapeDtypeStruct(shape, BF16),
            jax.ShapeDtypeStruct((9, C, C), F32),
            jax.ShapeDtypeStruct((3, C, C), F32),
        ),
        in_specs=[any_spec] * 3,
        out_specs=(any_spec,) * 4,
        scratch_shapes=[V((4, 2, 4, 4, 16, 384), BF16), V((12, C, C), F32), V((2,) + shape, BF16), DMA((2, 4)), DMA((4,))],
        compiler_params=pltpu.CompilerParams(vmem_limit_bytes=58 * 1024 * 1024),
        cost_estimate=pl.CostEstimate(flops=0, bytes_accessed=9_000_000, transcendentals=0),
    )(tout, ig, ag)
    return out_frames, in_grad, spatial_grad.reshape(3, 3, C, C), temporal_grad


def solution(mesh):
    frames = P("tm", "space", None, None)
    return jax.shard_map(
        section,
        mesh=mesh,
        in_specs=(frames, frames, P(), P(), P(), P(), P(), P()),
        out_specs=(frames, frames, P(), P()),
        check_vma=False,
    )
```
